32 devices in a mesh: grp: 2 (over y), ia: 8 (over z, x), ja: 2 (over core).
Axes of the slice: x: 2, y: 2, z: 4, core: 2. Of those that a mesh axis runs over, the one named last changes fastest.
Arguments:
- adjoint_temp: float32 [50, 32, 1024], P('grp', 'ja', 'ia'), parts along dimension 0
- adjoint_surface: float32 [64, 1024], P(('grp', 'ja'), 'ia'), parts along dimension 0, may hold values from -6 to 6
- trajectory_u: float32 [2, 25, 32, 1024], P(None, None, 'ja', 'ia'), may hold values from -6 to 6
- trajectory_v: float32 [2, 25, 32, 1024], P(None, None, 'ja', 'ia'), may hold values from -6 to 6
- levels: int32 [32, 1024], P('ja', 'ia'), may hold values from 0 to 25, as said below
- partner: int32 [1024], P('ia'), may hold values from 0 to 1023, as said below
- thickness: float32 [25], replicated, may hold values from 0.2 to 1
- coupling: float32 [25], replicated, may hold values from 0.2 to 1
Outputs:
- temp_gradient: float32 [50, 32, 1024], P('grp', 'ja', 'ia'), parts along dimension 0
- surface_gradient: float32 [64, 1024], P(('grp', 'ja'), 'ia'), parts along dimension 0
The draws below stay inside these ranges and needn't reach their ends.
There are 2 independent parts, one for each index of `grp`. The reference program is written for one: setup_inputs(seed, part) draws one part's arguments, and reference() takes and returns one part's arrays. A program takes and returns all parts, laid end to end along the dimension named above; an argument that names none is the same for every part. Nothing has to cross between parts.
Inputs may be any that keep to these rules, and one draw needn't show every extreme that they name: `levels`: 0 marks a land column. partner[partner[i]] = i and partner[i] != i for every column i.
All inputs are finite; a program needn't handle non-finite values.
Results may differ from the reference program's by a relative error of at most 0.0001.
Values sent between devices are 32-bit elements; how exact they have to be, the bound alone decides.
No kernel may reach another device: no remote copies, remote signals or barrier semaphores. Data moves between devices by JAX's collectives and lax.ppermute only.
A program may use at most 64 MiB of HBM per device.

```python
import math
import jax
import jax.numpy as jnp

LEVELS = 25
STEPS = 2
SOLVER_ITERS = 2
NI = 1024
NJ = 32


def draw_levels(key, part):
    land_key = jax.random.fold_in(key, 11)
    depth_key = jax.random.fold_in(key, 12)
    land = jax.random.randint(land_key, (NJ, NI), 0, 4)
    depth = jax.random.randint(depth_key, (NJ, NI), 1, LEVELS + 1)
    return jnp.where(land == 0, 0, depth).astype(jnp.int32)


def draw_partner(key, part):
    order = jax.random.permutation(jax.random.fold_in(key, 21), NI).astype(jnp.int32)
    first_half = order[0::2]
    second_half = order[1::2]
    table = jnp.zeros((NI,), dtype=jnp.int32)
    table = table.at[first_half].set(second_half)
    table = table.at[second_half].set(first_half)
    return table.astype(jnp.int32)


def draw_adjoint_temp(key, part):
    value_key = jax.random.fold_in(key, 31)
    rising = 1.0 + 2.0 * jnp.arange(NI, dtype=jnp.float32) / max(NI - 1, 1)
    values = jax.random.normal(value_key, (LEVELS, NJ, NI), jnp.float32)
    return jnp.clip(values, -6.0, 6.0) * rising


def shard_levels(rng, dims, pieces, least, largest):
    def one(dim, parts):
        heights = jax.random.uniform(jax.random.fold_in(jax.random.fold_in(rng, 6), dim), (parts,), jnp.float32, least / len(pieces), largest / len(pieces))
        return jnp.repeat(jnp.exp(heights), dims[dim] // parts).reshape((-1,) + (1,) * (len(dims) - dim - 1))

    gain = one(*pieces[0])
    for cut in pieces[1:]:
        gain = gain * one(*cut)
    return gain


def gaussian(rng, extent, width, reach, pieces=(), kind=jnp.bfloat16):
    array = width * jax.random.normal(rng, extent, jnp.float32)
    if pieces:
        array = array * shard_levels(rng, extent, pieces, -0.22, 0.18)
    return jnp.clip(array, -reach, reach).astype(kind)


def setup_inputs(seed: int = 0, part: int = 0) -> dict:
    keys = jax.random.split(jax.random.key(seed), 9)
    own_keys = jax.random.split(jax.random.fold_in(keys[8], part), 9)
    adjoint_temp = draw_adjoint_temp(jax.random.fold_in(jax.random.fold_in(keys[8], part), 71), part)
    adjoint_surface = gaussian(own_keys[1], (NJ, NI), 1.0, 6.0, ((0, 2), (1, 8)), jnp.float32)
    trajectory_u = gaussian(keys[2], (STEPS, LEVELS, NJ, NI), 1.0, 6.0, ((2, 2), (3, 8)), jnp.float32)
    trajectory_v = gaussian(keys[3], (STEPS, LEVELS, NJ, NI), 1.0, 6.0, ((2, 2), (3, 8)), jnp.float32)
    levels = draw_levels(jax.random.fold_in(keys[8], 71), part)
    partner = draw_partner(jax.random.fold_in(keys[8], 71), part)
    thickness = jnp.clip(jnp.exp(jax.random.uniform(keys[6], (LEVELS,), jnp.float32, math.log(0.2), math.log(1.0))), 0.2, 1.0)
    coupling = jnp.clip(jax.random.uniform(keys[7], (LEVELS,), jnp.float32, 0.2, 1.0), 0.2, 1.0)
    return {"adjoint_temp": adjoint_temp, "adjoint_surface": adjoint_surface, "trajectory_u": trajectory_u, "trajectory_v": trajectory_v, "levels": levels, "partner": partner, "thickness": thickness, "coupling": coupling}


time_step = 0.5
surface_coef = 2.0


def ocean_mask(levels):
    level_index = jnp.arange(LEVELS, dtype=jnp.int32)[:, None, None]
    return (level_index < levels[None]).astype(jnp.float32)


def face_weights(velocity_u, velocity_v, ocean):
    eastward = 0.5 * velocity_u * ocean * jnp.roll(ocean, -1, axis=2)
    upper = jnp.concatenate([ocean[:, 1:], ocean[:, -1:]], axis=1)
    northward = 0.5 * velocity_v * ocean * upper
    return eastward, northward


def surface_apply(field, partner):
    east_cells = jnp.roll(field, -1, axis=1)
    west_cells = jnp.roll(field, 1, axis=1)
    north_cells = jnp.concatenate([field[1:], field[-1:][:, partner]], axis=0)
    south_cells = jnp.concatenate([jnp.zeros_like(field[:1]), field[:-1]], axis=0)
    return (1.0 + 4.0 * surface_coef) * field - surface_coef * (east_cells + west_cells + north_cells + south_cells)


def surface_solve(forcing, partner):
    iterate = jnp.zeros_like(forcing)
    residual = forcing
    direction = forcing
    norm_now = jnp.sum(residual * residual)
    for sweep in range(SOLVER_ITERS):
        applied = surface_apply(direction, partner)
        step_size = norm_now / jnp.sum(direction * applied)
        iterate = iterate + step_size * direction
        if sweep + 1 < SOLVER_ITERS:
            residual = residual - step_size * applied
            norm_next = jnp.sum(residual * residual)
            direction = residual + (norm_next / norm_now) * direction
            norm_now = norm_next
    return iterate


def advect_adjoint(adjoint_mid, ocean, eastward, northward, partner):
    scaled = time_step * ocean * adjoint_mid
    east_cells = jnp.roll(scaled, -1, axis=2)
    west_cells = jnp.roll(scaled, 1, axis=2)
    zero_row = jnp.zeros_like(scaled[:, :1])
    north_cells = jnp.concatenate([scaled[:, 1:], zero_row], axis=1)
    south_cells = jnp.concatenate([zero_row, scaled[:, :-1]], axis=1)
    west_face = jnp.roll(eastward, 1, axis=2)
    south_face = jnp.concatenate([jnp.zeros_like(northward[:, :1]), northward[:, :-1]], axis=1)
    result = adjoint_mid + eastward * (east_cells - scaled) + west_face * (scaled - west_cells)
    result = result + northward * (north_cells - scaled) + south_face * (scaled - south_cells)
    across = northward[:, -1, :] * scaled[:, -1, :]
    return result.at[:, -1, :].add(-across[:, partner])


def reference(adjoint_temp, adjoint_surface, trajectory_u, trajectory_v, levels, partner, thickness, coupling):
    ocean = ocean_mask(levels)
    temp_gradient = adjoint_temp
    surface_gradient = adjoint_surface
    for step_index in range(STEPS - 1, -1, -1):
        eastward, northward = face_weights(trajectory_u[step_index], trajectory_v[step_index], ocean)
        forcing = surface_gradient + jnp.sum(coupling[:, None, None] * ocean * temp_gradient, axis=0)
        solved = surface_solve(forcing, partner)
        adjoint_mid = temp_gradient + thickness[:, None, None] * ocean * solved[None]
        temp_gradient = advect_adjoint(adjoint_mid, ocean, eastward, northward, partner)
        surface_gradient = solved
    return temp_gradient, surface_gradient
```

```python
import jax
import jax.numpy as jnp
from jax import lax
from jax.experimental import pallas as pl
from jax.experimental.pallas import tpu as pltpu
from jax.sharding import PartitionSpec as P

SOLVER_ITERS = 2
SURFACE_COEF = 2.0
F32 = jnp.float32

PART1, LEV1, V1ROW, EDGE1, ROWS1 = 16, 17, 18, 48, 64
HROW2, G2ROW, T2ROW, EDGE2, ROWS2 = 16, 17, 42, 72, 88
SHARED = 24
PEER1, PEER2 = 80, 32


def iota(shape, dim):
    return lax.broadcasted_iota(jnp.int32, shape, dim)


def full_sum(x):
    return jnp.sum(jnp.sum(x, axis=0), axis=(0, 1), keepdims=True)


def fold_take(values, block, lane):
    out = jnp.zeros(block.shape, F32)
    for b in range(values.shape[0]):
        source = jnp.broadcast_to(values[b : b + 1], block.shape)
        out = jnp.where(block == b, jnp.take_along_axis(source, lane, axis=1), out)
    return out


def shift_blocks(x, step):
    return jnp.concatenate([x[step:], x[:step]], axis=0)


def surface_apply(field, block, lane):
    n, rows, cols = field.shape
    col = iota(field.shape, 2)
    row = iota(field.shape, 1)
    left = pltpu.roll(field, 1, 2)
    right = pltpu.roll(field, cols - 1, 2)
    west = jnp.where(col == 0, shift_blocks(left, n - 1), left)
    east = jnp.where(col == cols - 1, shift_blocks(right, 1), right)
    across = fold_take(field[:, rows - 1, :], block, lane)
    north = jnp.where(row == rows - 1, across[:, None, :], pltpu.roll(field, rows - 1, 1))
    south = jnp.where(row == 0, 0.0, pltpu.roll(field, 1, 1))
    return (1.0 + 4.0 * SURFACE_COEF) * field - SURFACE_COEF * (east + west + north + south)


def surface_solve(forcing, block, lane):
    residual = forcing
    direction = forcing
    iterate = None
    norm_now = full_sum(residual * residual)
    for sweep in range(SOLVER_ITERS):
        applied = surface_apply(direction, block, lane)
        step_size = norm_now / full_sum(direction * applied)
        part = step_size * direction
        iterate = part if iterate is None else iterate + part
        if sweep + 1 < SOLVER_ITERS:
            residual = residual - step_size * applied
            norm_next = full_sum(residual * residual)
            direction = residual + norm_next / norm_now * direction
            norm_now = norm_next
    return iterate


def level_rows(ref, base, count, rows):
    return ref[pl.ds(base, count, stride=rows), :]


def pack_kernel(cp, adj, surf, u, v, lev, par, out, peer):
    rows, cols = surf.shape
    count = adj.shape[0] // rows
    top = lax.axis_index("ja") == lax.axis_size("ja") - 1
    lane = iota((rows, cols), 1)
    depth = lev[...].astype(F32)
    forcing = surf[...]
    last, first = cols - 1, 0
    edge = jnp.where(lane == 4 * count, depth[:, last:], 0.0)
    edge = jnp.where(lane == 4 * count + 1, depth[:, :1], edge)
    for k in range(count):
        here = adj[k * rows : (k + 1) * rows, :]
        u0 = u[0, k * rows : (k + 1) * rows, :]
        u1 = u[1, k * rows : (k + 1) * rows, :]
        forcing = forcing + cp[k] * jnp.where(depth > k, here, 0.0)
        edge = jnp.where(lane == k, here[:, last:], edge)
        edge = jnp.where(lane == count + k, u1[:, last:], edge)
        edge = jnp.where(lane == 2 * count + k, u0[:, last:], edge)
        edge = jnp.where(lane == 3 * count + k, here[:, :1], edge)
    out[...] = jnp.zeros(out.shape, F32)
    out[0:rows, :] = forcing
    out[PART1 : PART1 + 1, :] = par[...].astype(F32)
    out[LEV1 : LEV1 + 1, :] = depth[rows - 1 :]
    out[EDGE1 : EDGE1 + rows, :] = edge
    peer[...] = jnp.zeros(peer.shape, F32)
    v0row = v[0, pl.ds(rows - 1, count, stride=rows), :]
    out[V1ROW : V1ROW + count, :] = v0row
    is_top = jnp.full((count, cols), top.astype(jnp.int32)) == 1
    peer[0:count, :] = jnp.where(
        is_top, level_rows(adj, 0, count, rows), level_rows(adj, rows - 1, count, rows)
    )
    peer[count : 2 * count, :] = v[1, pl.ds(rows - 1, count, stride=rows), :]
    peer[2 * count : 3 * count, :] = v0row
    peer[3 * count : 3 * count + 1, :] = jnp.where(is_top[:1], depth[:1], depth[rows - 1 :])


def whole_field(mine, other, rows, top):
    n, _, cols = mine.shape
    here = mine[:, 0:rows, :]
    there = other[0 : n * SHARED, :].reshape(n, SHARED, cols)[:, :rows, :]
    is_top = jnp.full(here.shape, top.astype(jnp.int32)) == 1
    low = jnp.where(is_top, there, here)
    high = jnp.where(is_top, here, there)
    return jnp.concatenate([low, high], axis=1)


def top_row(mine, other, index, top):
    n, _, cols = mine.shape
    is_top = jnp.full((n, cols), top.astype(jnp.int32)) == 1
    there = other[pl.ds(index, n, stride=SHARED), :]
    return jnp.where(is_top, mine[:, index, :], there)


def position(n):
    me = lax.axis_index("ia")
    return me, lax.rem(me + n - 1, n), lax.rem(me + 1, n)


def sweep_levels(count, rows, th, fetch, west_of, east_of, u, v, pieces, top, depth, masks, emit):
    own, left, right, beside, beside_temp, beside_v = pieces
    east_depth, west_depth, north_depth, south_depth = masks
    cols = own.shape[1]
    lane = iota((rows, cols), 1)
    row = iota((rows, cols), 0)
    is_top = jnp.full((1, cols), top.astype(jnp.int32)) == 1
    for k in range(count):
        here = fetch(k)
        add = th[k] * own
        mid = here + jnp.where(depth > k, add, 0.0)
        bare = here + add
        u_west, t_west = west_of(k)
        west_value = t_west + th[k] * left
        east_value = jnp.where(
            lane == cols - 1, east_of(k) + th[k] * right, pltpu.roll(bare, cols - 1, 1)
        )
        u_here = u[k * rows : (k + 1) * rows, :]
        v_here = v[k * rows : (k + 1) * rows, :]
        flux_east = jnp.where(east_depth > k, 0.25 * u_here * (east_value - bare), 0.0)
        flux_first = jnp.where(west_depth > k, 0.25 * u_west * (bare - west_value), 0.0)
        flux_west = jnp.where(lane == 0, flux_first, pltpu.roll(flux_east, 1, 1))
        beside_value = beside_temp(k) + th[k] * beside
        above = jnp.where(is_top, 0.0, beside_value)
        north_value = jnp.where(row == rows - 1, above, pltpu.roll(bare, rows - 1, 0))
        flux_north = jnp.where(north_depth > k, 0.25 * v_here * (north_value - bare), 0.0)
        flux_below = jnp.where(south_depth > k, 0.25 * beside_v(k) * (bare[:1] - beside_value), 0.0)
        flux_south = jnp.where(row == 0, flux_below, pltpu.roll(flux_north, 1, 0))
        emit(k, mid + flux_east + flux_west + flux_north + flux_south, flux_north)


def face_depths(depth, edge_left, edge_right, beside_depth, count, top):
    rows, cols = depth.shape
    lane = iota(depth.shape, 1)
    row = iota(depth.shape, 0)
    is_top = jnp.full(depth.shape, top.astype(jnp.int32)) == 1
    right = edge_right[:, 4 * count + 1 : 4 * count + 2]
    east = jnp.minimum(depth, jnp.where(lane == cols - 1, right, pltpu.roll(depth, cols - 1, 1)))
    west = jnp.minimum(depth, edge_left[:, 4 * count : 4 * count + 1])
    above = jnp.where(is_top, depth, beside_depth)
    north = jnp.minimum(depth, jnp.where(row == rows - 1, above, pltpu.roll(depth, rows - 1, 0)))
    south = jnp.where(is_top[:1], jnp.minimum(depth[:1], beside_depth), 0.0)
    return east, west, north, south


def load_pieces(solved, me, west, east, rows, top):
    cols = solved.shape[-1]
    here = pl.ds(pl.multiple_of(jnp.where(top, rows, 0), 8), rows)
    own = solved[me, here, :]
    left = pltpu.roll(solved[west, here, :], 1, 1)
    right = pltpu.roll(solved[east, here, :], cols - 1, 1)
    is_top = jnp.full((1, cols), top.astype(jnp.int32)) == 1
    block = solved[me]
    beside = jnp.where(is_top, block[rows - 1 : rows], block[rows : rows + 1])
    return own, left, right, beside


def first_kernel(cp, th, mine, other, adj, u, v, lev, t_out, out, peer, solved, rowbuf):
    n, _, cols = mine.shape
    rows = lev.shape[0]
    count = adj.shape[0] // rows
    top = lax.axis_index("ja") == lax.axis_size("ja") - 1
    me, west, east = position(n)
    partner = mine[:, PART1, :].astype(jnp.int32)
    block, lane = partner >> 7, partner & 127
    forcing = whole_field(mine, other, rows, top)
    solved[...] = surface_solve(forcing, block, lane)
    rowbuf[...] = fold_take(top_row(mine, other, LEV1, top), block, lane)
    across_depth = rowbuf[pl.ds(me, 1), :]
    depth = lev[...].astype(F32)
    edge_left = mine[west, EDGE1 : EDGE1 + rows, :]
    edge_right = mine[east, EDGE1 : EDGE1 + rows, :]
    base = n * SHARED
    beside_depth = other[base + 3 * count : base + 3 * count + 1, :]
    masks = face_depths(depth, edge_left, edge_right, beside_depth, count, top)
    own, left, right, beside = load_pieces(solved, me, west, east, rows, top)
    pieces = (
        own,
        left,
        right,
        beside,
        lambda k: other[base + k : base + k + 1, :],
        lambda k: other[base + count + k : base + count + k + 1, :],
    )
    out[...] = jnp.zeros(out.shape, F32)
    peer[...] = jnp.zeros(peer.shape, F32)
    spot = iota((rows, cols), 1)
    is_top = jnp.full((1, cols), top.astype(jnp.int32)) == 1
    carry = {
        "forcing": own,
        "edge": jnp.zeros((rows, cols), F32),
        "fold": jnp.zeros((1, cols), F32),
    }

    def emit(k, value, flux_north):
        t_out[k * rows : (k + 1) * rows, :] = value
        carry["forcing"] = carry["forcing"] + cp[k] * jnp.where(depth > k, value, 0.0)
        edge = jnp.where(spot == k, value[:, cols - 1 :], carry["edge"])
        carry["edge"] = jnp.where(spot == count + k, value[:, :1], edge)
        fold = -flux_north[rows - 1 :]
        carry["fold"] = carry["fold"] + cp[k] * jnp.where(across_depth > k, fold, 0.0)
        out[G2ROW + k : G2ROW + k + 1, :] = fold
        out[T2ROW + k : T2ROW + k + 1, :] = value[rows - 1 :]
        peer[k : k + 1, :] = jnp.where(is_top, value[:1], value[rows - 1 :])

    sweep_levels(
        count,
        rows,
        th,
        lambda k: adj[k * rows : (k + 1) * rows, :],
        lambda k: (edge_left[:, count + k : count + k + 1], edge_left[:, k : k + 1]),
        lambda k: edge_right[:, 3 * count + k : 3 * count + k + 1],
        u.at[1],
        v.at[1],
        pieces,
        top,
        depth,
        masks,
        emit,
    )
    out[0:rows, :] = carry["forcing"]
    out[HROW2 : HROW2 + 1, :] = carry["fold"]
    out[EDGE2 : EDGE2 + rows, :] = carry["edge"]


def second_kernel(
    th, mine, other, mine1, other1, temp, u, v, lev, t_out, s_out, solved, rowbuf, rowbuf2
):
    n, _, cols = mine.shape
    rows = lev.shape[0]
    count = temp.shape[0] // rows
    top = lax.axis_index("ja") == lax.axis_size("ja") - 1
    me, west, east = position(n)
    partner = mine1[:, PART1, :].astype(jnp.int32)
    block, lane = partner >> 7, partner & 127
    forcing = whole_field(mine, other, rows, top)
    fold = fold_take(top_row(mine, other, HROW2, top), block, lane)
    row3 = iota(forcing.shape, 1)
    forcing = forcing - jnp.where(row3 == 2 * rows - 1, fold[:, None, :], 0.0)
    iterate = surface_solve(forcing, block, lane)
    solved[...] = iterate
    rowbuf[...] = fold_take(top_row(mine1, other1, LEV1, top), block, lane)
    rowbuf2[...] = fold_take(iterate[:, 2 * rows - 1, :], block, lane)
    across_depth = rowbuf[pl.ds(me, 1), :]
    across_solved = rowbuf2[pl.ds(me, 1), :]

    tall = 32
    spot = iota((1, cols), 1)
    own_partner = mine1[me, PART1 : PART1 + 1, :].astype(jnp.int32)
    beside_left = pltpu.roll(mine1[west, PART1 : PART1 + 8, :], 1, 1)[:1].astype(jnp.int32)
    beside_right = pltpu.roll(mine1[east, PART1 : PART1 + 8, :], cols - 1, 1)[:1].astype(jnp.int32)
    end_partner = jnp.where(spot == 0, beside_left, beside_right)
    end_partner = jnp.where((spot == 0) | (spot == cols - 1), end_partner, 0)
    own_partner = jnp.broadcast_to(own_partner, (tall, cols))
    end_partner = jnp.broadcast_to(end_partner, (tall, cols))
    own_block, own_lane = own_partner >> 7, own_partner & 127
    end_block, end_lane = end_partner >> 7, end_partner & 127
    zero = jnp.zeros((tall, cols), F32)
    fold_own, fold_end, temp_across, v_across = zero, zero, zero, zero
    for b in range(n):
        flux = mine[b, G2ROW : G2ROW + tall, :]
        here = own_block == b
        fold_own = jnp.where(here, jnp.take_along_axis(flux, own_lane, axis=1), fold_own)
        fold_end = jnp.where(
            end_block == b, jnp.take_along_axis(flux, end_lane, axis=1), fold_end
        )
        line = mine[b, T2ROW : T2ROW + tall, :]
        temp_across = jnp.where(here, jnp.take_along_axis(line, own_lane, axis=1), temp_across)
        speed = mine1[b, V1ROW : V1ROW + tall, :]
        v_across = jnp.where(here, jnp.take_along_axis(speed, own_lane, axis=1), v_across)
    level = iota((tall, cols), 0)
    weight = zero
    for k in range(count):
        weight = jnp.where(level == k, th[k], weight)
    sent = mine[me, G2ROW : G2ROW + tall, :]
    fold_last = jnp.where(
        across_depth > level.astype(F32),
        0.25 * v_across * (temp_across - sent + weight * across_solved),
        0.0,
    )

    depth = lev[...].astype(F32)
    edge1_left = mine1[west, EDGE1 : EDGE1 + rows, :]
    edge1_right = mine1[east, EDGE1 : EDGE1 + rows, :]
    edge_left = mine[west, EDGE2 : EDGE2 + rows, :]
    edge_right = mine[east, EDGE2 : EDGE2 + rows, :]
    base, base1 = n * SHARED, n * SHARED
    beside_depth = other1[base1 + 3 * count : base1 + 3 * count + 1, :]
    masks = face_depths(depth, edge1_left, edge1_right, beside_depth, count, top)
    own, left, right, beside = load_pieces(solved, me, west, east, rows, top)
    s_out[...] = own
    pieces = (
        own,
        left,
        right,
        beside,
        lambda k: other[base + k : base + k + 1, :],
        lambda k: other1[base1 + 2 * count + k : base1 + 2 * count + k + 1, :],
    )
    row = iota((rows, cols), 0)
    on_fold = (row == rows - 1) & (jnp.full((rows, cols), top.astype(jnp.int32)) == 1)

    def less(value, lines, k):
        return value - jnp.where(on_fold, lines[k : k + 1], 0.0)

    def emit(k, value, flux_north):
        t_out[k * rows : (k + 1) * rows, :] = less(value, fold_last, k)

    sweep_levels(
        count,
        rows,
        th,
        lambda k: less(temp[k * rows : (k + 1) * rows, :], fold_own, k),
        lambda k: (
            edge1_left[:, 2 * count + k : 2 * count + k + 1],
            less(jnp.broadcast_to(edge_left[:, k : k + 1], (rows, cols)), fold_end, k),
        ),
        lambda k: less(
            jnp.broadcast_to(edge_right[:, count + k : count + k + 1], (rows, cols)), fold_end, k
        ),
        u.at[0],
        v.at[0],
        pieces,
        top,
        depth,
        masks,
        emit,
    )


def gather_columns(block):
    n = lax.axis_size("ia")
    me = lax.axis_index("ia")
    y = block
    dim = 0
    step = n // 2
    while step:
        z = lax.ppermute(y, "ia", [(i, i ^ step) for i in range(n)])
        odd = (me // step) % 2 == 1
        y = jnp.where(odd, jnp.stack([z, y], axis=dim), jnp.stack([y, z], axis=dim))
        dim += 1
        step //= 2
    return y.reshape((n,) + block.shape)


def swap_cores(gathered, peer):
    n, _, cols = gathered.shape
    shared = gathered[:, :SHARED, :].reshape(n * SHARED, cols)
    return lax.ppermute(jnp.concatenate([shared, peer]), "ja", [(0, 1), (1, 0)])


def on_device(
    adjoint_temp, adjoint_surface, trajectory_u, trajectory_v, levels, partner, thickness, coupling
):
    steps, count, rows, cols = trajectory_u.shape
    n = lax.axis_size("ia")
    flat = count * rows
    adj = adjoint_temp.reshape(flat, cols)
    u = trajectory_u.reshape(steps, flat, cols)
    v = trajectory_v.reshape(steps, flat, cols)
    par = partner.reshape(1, cols)
    smem = pl.BlockSpec(memory_space=pltpu.SMEM)
    vmem = pl.BlockSpec(memory_space=pltpu.VMEM)

    def shape(*dims):
        return jax.ShapeDtypeStruct(dims, F32)

    out, peer = pl.pallas_call(
        pack_kernel,
        out_shape=(shape(ROWS1, cols), shape(PEER1, cols)),
        in_specs=[smem] + [vmem] * 6,
        out_specs=(vmem, vmem),
    )(coupling, adj, adjoint_surface, u, v, levels, par)
    mine1 = gather_columns(out)
    other1 = swap_cores(mine1, peer)
    temp, out, peer = pl.pallas_call(
        first_kernel,
        out_shape=(shape(flat, cols), shape(ROWS2, cols), shape(PEER2, cols)),
        in_specs=[smem, smem] + [vmem] * 6,
        out_specs=(vmem, vmem, vmem),
        scratch_shapes=[pltpu.VMEM((n, 2 * rows, cols), F32), pltpu.VMEM((n, cols), F32)],
    )(coupling, thickness, mine1, other1, adj, u, v, levels)
    mine = gather_columns(out)
    other = swap_cores(mine, peer)
    temp_gradient, surface_gradient = pl.pallas_call(
        second_kernel,
        out_shape=(shape(flat, cols), shape(rows, cols)),
        in_specs=[smem] + [vmem] * 8,
        out_specs=(vmem, vmem),
        scratch_shapes=[
            pltpu.VMEM((n, 2 * rows, cols), F32),
            pltpu.VMEM((n, cols), F32),
            pltpu.VMEM((n, cols), F32),
        ],
    )(thickness, mine, other, mine1, other1, temp, u, v, levels)
    return temp_gradient.reshape(count, rows, cols), surface_gradient


def solution(mesh):
    return jax.shard_map(
        on_device,
        mesh=mesh,
        in_specs=(
            P("grp", "ja", "ia"),
            P(("grp", "ja"), "ia"),
            P(None, None, "ja", "ia"),
            P(None, None, "ja", "ia"),
            P("ja", "ia"),
            P("ia"),
            P(),
            P(),
        ),
        out_specs=(P("grp", "ja", "ia"), P(("grp", "ja"), "ia")),
        check_vma=False,
    )
```

```python
import jax
import jax.numpy as jnp
from jax import lax
from jax.experimental import pallas as pl
from jax.experimental.pallas import tpu as pltpu
from jax.sharding import PartitionSpec as P

SOLVER_ITERS = 2
SURFACE_COEF = 2.0
F32 = jnp.float32

EDGE1, PART1, LEV1, ROWS1 = 16, 32, 33, 40
EDGE2, HROW2, LINE2, FLUX2, ROWS2 = 16, 24, 25, 50, 64
PEER1, PEER2 = 104, 32
WINDOW = 16
TALL = 32


def iota(shape, dim):
    return lax.broadcasted_iota(jnp.int32, shape, dim)


def full_sum(x):
    return jnp.sum(jnp.sum(x, axis=0), axis=(0, 1), keepdims=True)


def split_index(column, cols):
    return column >> (cols.bit_length() - 1), column & (cols - 1)


def fold_take(values, block, lane):
    out = jnp.zeros(block.shape, F32)
    for b in range(values.shape[0]):
        source = jnp.broadcast_to(values[b : b + 1], block.shape)
        out = jnp.where(block == b, jnp.take_along_axis(source, lane, axis=1), out)
    return out


def shift_blocks(x, step):
    return jnp.concatenate([x[step:], x[:step]], axis=0)


def surface_apply(field, block, lane):
    n, rows, cols = field.shape
    col = iota(field.shape, 2)
    row = iota(field.shape, 1)
    left = pltpu.roll(field, 1, 2)
    right = pltpu.roll(field, cols - 1, 2)
    west = jnp.where(col == 0, shift_blocks(left, n - 1), left)
    east = jnp.where(col == cols - 1, shift_blocks(right, 1), right)
    across = fold_take(field[:, rows - 1, :], block, lane)
    north = jnp.where(row == rows - 1, across[:, None, :], pltpu.roll(field, rows - 1, 1))
    south = jnp.where(row == 0, 0.0, pltpu.roll(field, 1, 1))
    return (1.0 + 4.0 * SURFACE_COEF) * field - SURFACE_COEF * (east + west + north + south)


def surface_solve(forcing, block, lane):
    residual = forcing
    direction = forcing
    iterate = None
    norm_now = full_sum(residual * residual)
    for sweep in range(SOLVER_ITERS):
        applied = surface_apply(direction, block, lane)
        step_size = norm_now / full_sum(direction * applied)
        part = step_size * direction
        iterate = part if iterate is None else iterate + part
        if sweep + 1 < SOLVER_ITERS:
            residual = residual - step_size * applied
            norm_next = full_sum(residual * residual)
            direction = residual + norm_next / norm_now * direction
            norm_now = norm_next
    return iterate


def level_rows(ref, base, count, rows):
    return ref[pl.ds(base, count, stride=rows), :]


def pack_kernel(cp, adj, surf, u, v, lev, par, out, peer):
    rows, cols = surf.shape
    count = adj.shape[0] // rows
    top = lax.axis_index("ja") == lax.axis_size("ja") - 1
    lane = iota((rows, cols), 1)
    depth = lev[...].astype(F32)
    forcing = surf[...]
    last, first = cols - 1, 0
    edge = jnp.where(lane == 4 * count, depth[:, last:], 0.0)
    edge = jnp.where(lane == 4 * count + 1, depth[:, :1], edge)
    for k in range(count):
        here = adj[k * rows : (k + 1) * rows, :]
        u0 = u[0, k * rows : (k + 1) * rows, :]
        u1 = u[1, k * rows : (k + 1) * rows, :]
        forcing = forcing + cp[k] * jnp.where(depth > k, here, 0.0)
        edge = jnp.where(lane == k, here[:, last:], edge)
        edge = jnp.where(lane == count + k, u1[:, last:], edge)
        edge = jnp.where(lane == 2 * count + k, u0[:, last:], edge)
        edge = jnp.where(lane == 3 * count + k, here[:, :1], edge)
    out[0:rows, :] = forcing
    out[EDGE1 : EDGE1 + rows, :] = edge
    out[PART1:ROWS1, :] = jnp.zeros((ROWS1 - PART1, cols), F32)
    out[PART1 : PART1 + 1, :] = par[...].astype(F32)
    out[LEV1 : LEV1 + 1, :] = depth[rows - 1 :]
    peer[...] = jnp.zeros(peer.shape, F32)
    is_top = jnp.full((count, cols), top.astype(jnp.int32)) == 1
    last_row = level_rows(adj, rows - 1, count, rows)
    peer[0:count, :] = jnp.where(is_top, level_rows(adj, 0, count, rows), last_row)
    peer[count : 2 * count, :] = v[1, pl.ds(rows - 1, count, stride=rows), :]
    peer[2 * count : 3 * count, :] = v[0, pl.ds(rows - 1, count, stride=rows), :]
    peer[3 * count : 4 * count, :] = last_row
    peer[4 * count : 4 * count + 1, :] = jnp.where(is_top[:1], depth[:1], depth[rows - 1 :])


def parity(x):
    for shift in (16, 8, 4, 2, 1):
        x = x ^ (x >> shift)
    return x & 1


class Messages:
    def __init__(self, both):
        self.both = both
        self.count = both.shape[1]
        self.cols = both.shape[3]
        self.me = lax.axis_index("ia")
        self.core = lax.axis_index("ja")

    def place(self, block, core):
        return core ^ self.core ^ parity(block ^ self.me)

    def part(self, block, core, start, stop):
        return self.both[self.place(block, core), block, start:stop, :]

    def field(self, rows):
        blocks = [
            jnp.concatenate([self.part(b, 0, 0, rows), self.part(b, 1, 0, rows)], axis=0)
            for b in range(self.count)
        ]
        return jnp.stack(blocks, axis=0)

    def line(self, index):
        return self.both[0, :, index, :]

    def top_line(self, index):
        block = iota((self.count, self.cols), 0)
        here = (1 ^ self.core ^ parity(block ^ self.me)) == 0
        return jnp.where(here, self.both[0, :, index, :], self.both[1, :, index, :])


def level_column(values, count, cols):
    level = iota((TALL, cols), 0)
    out = jnp.zeros((TALL, cols), F32)
    for k in range(count):
        out = jnp.where(level == k, values[k], out)
    return out


def position(n):
    me = lax.axis_index("ia")
    return me, lax.rem(me + n - 1, n), lax.rem(me + 1, n)


def sweep_levels(count, rows, th, fetch, west_of, east_of, u, v, pieces, top, depth, masks, emit):
    own, left, right, beside, beside_temp, beside_v = pieces
    east_depth, west_depth, north_depth, south_depth = masks
    cols = own.shape[1]
    lane = iota((rows, cols), 1)
    row = iota((rows, cols), 0)
    is_top = jnp.full((1, cols), top.astype(jnp.int32)) == 1
    for k in range(count):
        here = fetch(k)
        add = th[k] * own
        mid = here + jnp.where(depth > k, add, 0.0)
        bare = here + add
        u_west, t_west = west_of(k)
        west_value = t_west + th[k] * left
        east_value = jnp.where(
            lane == cols - 1, east_of(k) + th[k] * right, pltpu.roll(bare, cols - 1, 1)
        )
        u_here = u[k * rows : (k + 1) * rows, :]
        v_here = v[k * rows : (k + 1) * rows, :]
        flux_east = jnp.where(east_depth > k, 0.25 * u_here * (east_value - bare), 0.0)
        flux_first = jnp.where(west_depth > k, 0.25 * u_west * (bare - west_value), 0.0)
        flux_west = jnp.where(lane == 0, flux_first, pltpu.roll(flux_east, 1, 1))
        beside_value = beside_temp(k) + th[k] * beside
        above = jnp.where(is_top, 0.0, beside_value)
        north_value = jnp.where(row == rows - 1, above, pltpu.roll(bare, rows - 1, 0))
        flux_north = jnp.where(north_depth > k, 0.25 * v_here * (north_value - bare), 0.0)
        flux_below = jnp.where(south_depth > k, 0.25 * beside_v(k) * (bare[:1] - beside_value), 0.0)
        flux_south = jnp.where(row == 0, flux_below, pltpu.roll(flux_north, 1, 0))
        emit(k, mid + flux_east + flux_west + flux_north + flux_south)


def face_depths(depth, edge_left, edge_right, beside_depth, count, top):
    rows, cols = depth.shape
    lane = iota(depth.shape, 1)
    row = iota(depth.shape, 0)
    is_top = jnp.full(depth.shape, top.astype(jnp.int32)) == 1
    right = edge_right[:, 4 * count + 1 : 4 * count + 2]
    east = jnp.minimum(depth, jnp.where(lane == cols - 1, right, pltpu.roll(depth, cols - 1, 1)))
    west = jnp.minimum(depth, edge_left[:, 4 * count : 4 * count + 1])
    above = jnp.where(is_top, depth, beside_depth)
    north = jnp.minimum(depth, jnp.where(row == rows - 1, above, pltpu.roll(depth, rows - 1, 0)))
    south = jnp.where(is_top[:1], jnp.minimum(depth[:1], beside_depth), 0.0)
    return east, west, north, south


def load_pieces(solved, me, west, east, rows, top):
    cols = solved.shape[-1]
    here = pl.ds(pl.multiple_of(jnp.where(top, rows, 0), 8), rows)
    own = solved[me, here, :]
    left = pltpu.roll(solved[west, here, :], 1, 1)
    right = pltpu.roll(solved[east, here, :], cols - 1, 1)
    is_top = jnp.full((1, cols), top.astype(jnp.int32)) == 1
    block = solved[me]
    beside = jnp.where(is_top, block[rows - 1 : rows], block[rows : rows + 1])
    return own, left, right, beside


def first_kernel(cp, th, both, beyond, adj, u, v, lev, t_out, out, peer, kept, solved, rowbuf, tall):
    rows, cols = lev.shape
    count = adj.shape[0] // rows
    top = lax.axis_index("ja") == lax.axis_size("ja") - 1
    sent = Messages(both)
    own_core = lax.axis_index("ja")
    me, west, east = position(sent.count)
    partner = sent.line(PART1).astype(jnp.int32)
    block, lane = split_index(partner, cols)
    solved[...] = surface_solve(sent.field(rows), block, lane)
    fold_depth = sent.top_line(LEV1)
    rowbuf[...] = fold_take(fold_depth, block, lane)
    across_depth = rowbuf[pl.ds(me, 1), :]
    rowbuf[...] = fold_depth
    fold_depth = rowbuf[pl.ds(me, 1), :]

    is_top = jnp.full((count, cols), top.astype(jnp.int32)) == 1
    level = iota((TALL, cols), 0).astype(F32)
    tall[0, 0:count, :] = jnp.where(
        is_top, level_rows(v.at[1], rows - 1, count, rows), beyond[count : 2 * count, :]
    )
    tall[1, 0:count, :] = jnp.where(
        is_top, level_rows(adj, rows - 1, count, rows), beyond[3 * count : 4 * count, :]
    )
    fold_solved = solved[me, 2 * rows - 8 :, :][7:]
    flux = jnp.where(
        fold_depth > level,
        0.25 * tall[0] * (tall[1] + level_column(th, count, cols) * fold_solved),
        0.0,
    )
    into = jnp.where(across_depth > level, level_column(cp, count, cols) * flux, 0.0)
    kept[0:TALL, :] = flux
    kept[TALL:, :] = jnp.broadcast_to(across_depth, (8, cols))
    out[HROW2 : HROW2 + 1, :] = jnp.sum(into, axis=0, keepdims=True)

    depth = lev[...].astype(F32)
    edge_left = sent.part(west, own_core, EDGE1, EDGE1 + rows)
    edge_right = sent.part(east, own_core, EDGE1, EDGE1 + rows)
    beside_depth = beyond[4 * count : 4 * count + 1, :]
    masks = face_depths(depth, edge_left, edge_right, beside_depth, count, top)
    own, left, right, beside = load_pieces(solved, me, west, east, rows, top)
    pieces = (
        own,
        left,
        right,
        beside,
        lambda k: beyond[k : k + 1, :],
        lambda k: beyond[count + k : count + k + 1, :],
    )
    spot = iota((rows, cols), 1)
    carry = {"forcing": own, "edge": jnp.zeros((rows, cols), F32)}

    def emit(k, value):
        t_out[k * rows : (k + 1) * rows, :] = value
        carry["forcing"] = carry["forcing"] + cp[k] * jnp.where(depth > k, value, 0.0)
        edge = jnp.where(spot == k, value[:, cols - 1 :], carry["edge"])
        carry["edge"] = jnp.where(spot == count + k, value[:, :1], edge)

    sweep_levels(
        count,
        rows,
        th,
        lambda k: adj[k * rows : (k + 1) * rows, :],
        lambda k: (edge_left[:, count + k : count + k + 1], edge_left[:, k : k + 1]),
        lambda k: edge_right[:, 3 * count + k : 3 * count + k + 1],
        u.at[1],
        v.at[1],
        pieces,
        top,
        depth,
        masks,
        emit,
    )
    out[0:rows, :] = carry["forcing"]
    half = rows // 2
    edge = carry["edge"]
    out[EDGE2 : EDGE2 + half, :] = jnp.where(
        spot[:half] < cols // 2, edge[:half], pltpu.roll(edge[half:], cols // 2, 1)
    )
    last_row = level_rows(t_out, rows - 1, count, rows)
    out[LINE2 : LINE2 + count, :] = jnp.where(is_top, last_row, beyond[2 * count : 3 * count, :])
    later, share = count // 2, count - count // 2
    out[FLUX2 : FLUX2 + share, :] = jnp.where(
        is_top[:share], kept[later:count, :], kept[0:share, :]
    )
    out[FLUX2 + share :, :] = jnp.zeros((ROWS2 - FLUX2 - share, cols), F32)
    peer[0:count, :] = jnp.where(is_top, level_rows(t_out, 0, count, rows), last_row)
    peer[count:, :] = jnp.zeros((peer.shape[0] - count, cols), F32)


def second_kernel(
    th, both, beyond, both1, beyond1, kept, temp, u, v, lev, t_out, s_out, solved, rowbuf, tall
):
    rows, cols = lev.shape
    count = temp.shape[0] // rows
    top = lax.axis_index("ja") == lax.axis_size("ja") - 1
    sent, sent1 = Messages(both), Messages(both1)
    own_core = lax.axis_index("ja")
    n = sent.count
    me, west, east = position(n)
    partner = sent1.line(PART1).astype(jnp.int32)
    block, lane = split_index(partner, cols)
    forcing = sent.field(rows)
    fold = fold_take(sent.line(HROW2), block, lane)
    row3 = iota(forcing.shape, 1)
    forcing = forcing - jnp.where(row3 == 2 * rows - 1, fold[:, None, :], 0.0)
    iterate = surface_solve(forcing, block, lane)
    solved[...] = iterate
    rowbuf[...] = fold_take(iterate[:, 2 * rows - 1, :], block, lane)
    across_solved = rowbuf[pl.ds(me, 1), :]

    spot = iota((1, cols), 1)
    rowbuf[...] = sent1.line(PART1)
    beside_left = pltpu.roll(rowbuf[pl.ds(west, 1), :], 1, 1)
    beside_right = pltpu.roll(rowbuf[pl.ds(east, 1), :], cols - 1, 1)
    end_partner = jnp.where(spot == 0, beside_left, beside_right)
    end_partner = jnp.where((spot == 0) | (spot == cols - 1), end_partner, 0.0)
    own_partner = jnp.broadcast_to(rowbuf[pl.ds(me, 1), :], (TALL, cols)).astype(jnp.int32)
    end_partner = jnp.broadcast_to(end_partner, (WINDOW, cols)).astype(jnp.int32)
    own_block, own_lane = split_index(own_partner, cols)
    end_block, end_lane = split_index(end_partner, cols)
    zero, low = jnp.zeros((TALL, cols), F32), jnp.zeros((WINDOW, cols), F32)
    temp_across, v_across = zero, zero
    own_flux, end_flux = [low, low], [low, low]
    for b in range(n):
        here, there = own_block == b, end_block == b
        line = sent.part(b, 1, LINE2, LINE2 + TALL)
        temp_across = jnp.where(here, jnp.take_along_axis(line, own_lane, axis=1), temp_across)
        line = sent.part(b, 0, LINE2, LINE2 + TALL)
        v_across = jnp.where(here, jnp.take_along_axis(line, own_lane, axis=1), v_across)
        for c in range(2):
            line = sent.part(b, c, ROWS2 - WINDOW, ROWS2)
            moved = jnp.take_along_axis(line, own_lane[:WINDOW], axis=1)
            own_flux[c] = jnp.where(here[:WINDOW], moved, own_flux[c])
            moved = jnp.take_along_axis(line, end_lane, axis=1)
            end_flux[c] = jnp.where(there, moved, end_flux[c])
    skip = FLUX2 - (ROWS2 - WINDOW)
    later, share = count // 2, count - count // 2
    for i, parts in enumerate((own_flux, end_flux)):
        for c, start in ((0, 0), (1, later)):
            tall[2, 0:WINDOW, :] = parts[c]
            tall[i, start : start + share, :] = tall[2, skip : skip + share, :]
    level = iota((TALL, cols), 0).astype(F32)
    fold_last = jnp.where(
        kept[TALL : TALL + 1, :] > level,
        0.25
        * v_across
        * (temp_across - kept[0:TALL, :] + level_column(th, count, cols) * across_solved),
        0.0,
    )
    tall[2] = fold_last

    depth = lev[...].astype(F32)
    edge1_left = sent1.part(west, own_core, EDGE1, EDGE1 + rows)
    edge1_right = sent1.part(east, own_core, EDGE1, EDGE1 + rows)
    half = rows // 2

    def both_rows(line):
        return jnp.concatenate([line, pltpu.roll(line, cols // 2, 1)], axis=0)

    edge_left = both_rows(sent.part(west, own_core, EDGE2, EDGE2 + half))
    edge_right = both_rows(sent.part(east, own_core, EDGE2, EDGE2 + half))
    beside_depth = beyond1[4 * count : 4 * count + 1, :]
    masks = face_depths(depth, edge1_left, edge1_right, beside_depth, count, top)
    own, left, right, beside = load_pieces(solved, me, west, east, rows, top)
    s_out[...] = own
    pieces = (
        own,
        left,
        right,
        beside,
        lambda k: beyond[k : k + 1, :],
        lambda k: beyond1[2 * count + k : 2 * count + k + 1, :],
    )
    row = iota((rows, cols), 0)
    on_fold = (row == rows - 1) & (jnp.full((rows, cols), top.astype(jnp.int32)) == 1)

    def less(value, index, k):
        return value - jnp.where(on_fold, tall[index, k : k + 1, :], 0.0)

    def emit(k, value):
        t_out[k * rows : (k + 1) * rows, :] = less(value, 2, k)

    def spread(column):
        return jnp.broadcast_to(column, (rows, cols))

    sweep_levels(
        count,
        rows,
        th,
        lambda k: less(temp[k * rows : (k + 1) * rows, :], 0, k),
        lambda k: (
            edge1_left[:, 2 * count + k : 2 * count + k + 1],
            less(spread(edge_left[:, k : k + 1]), 1, k),
        ),
        lambda k: less(spread(edge_right[:, count + k : count + k + 1]), 1, k),
        u.at[0],
        v.at[0],
        pieces,
        top,
        depth,
        masks,
        emit,
    )


def exchange(block, peer):
    n = lax.axis_size("ia")
    me = lax.axis_index("ia")
    rows, cols = block.shape
    y = block
    dim = 0
    step = n // 2
    while step:
        pairs = [(2 * i + c, 2 * (i ^ step) + (1 - c)) for i in range(n) for c in range(2)]
        z = lax.ppermute(y, ("ia", "ja"), pairs)
        odd = (me // step) % 2 == 1
        y = jnp.where(odd, jnp.stack([z, y], axis=dim), jnp.stack([y, z], axis=dim))
        dim += 1
        step //= 2
    y = y.reshape(n * rows, cols)
    z = lax.ppermute(jnp.concatenate([y, peer]), "ja", [(0, 1), (1, 0)])
    both = jnp.stack([y, z[: n * rows]]).reshape(2, n, rows, cols)
    return both, z[n * rows :]


def on_device(
    adjoint_temp, adjoint_surface, trajectory_u, trajectory_v, levels, partner, thickness, coupling
):
    steps, count, rows, cols = trajectory_u.shape
    n = lax.axis_size("ia")
    flat = count * rows
    adj = adjoint_temp.reshape(flat, cols)
    u = trajectory_u.reshape(steps, flat, cols)
    v = trajectory_v.reshape(steps, flat, cols)
    par = partner.reshape(1, cols)
    smem = pl.BlockSpec(memory_space=pltpu.SMEM)
    vmem = pl.BlockSpec(memory_space=pltpu.VMEM)

    def shape(*dims):
        return jax.ShapeDtypeStruct(dims, F32)

    small = pltpu.CompilerParams(vmem_limit_bytes=(8 + n // 2) * 2**20)
    out, peer = pl.pallas_call(
        pack_kernel,
        out_shape=(shape(ROWS1, cols), shape(PEER1, cols)),
        in_specs=[smem] + [vmem] * 6,
        out_specs=(vmem, vmem),
    )(coupling, adj, adjoint_surface, u, v, levels, par)
    both1, beyond1 = exchange(out, peer)
    temp, out, peer, kept = pl.pallas_call(
        first_kernel,
        out_shape=(
            shape(flat, cols),
            shape(ROWS2, cols),
            shape(PEER2, cols),
            shape(TALL + 8, cols),
        ),
        in_specs=[smem, smem] + [vmem] * 6,
        out_specs=(vmem,) * 4,
        scratch_shapes=[
            pltpu.VMEM((n, 2 * rows, cols), F32),
            pltpu.VMEM((n, cols), F32),
            pltpu.VMEM((2, TALL, cols), F32),
        ],
        compiler_params=small,
    )(coupling, thickness, both1, beyond1, adj, u, v, levels)
    both, beyond = exchange(out, peer)
    temp_gradient, surface_gradient = pl.pallas_call(
        second_kernel,
        out_shape=(shape(flat, cols), shape(rows, cols)),
        in_specs=[smem] + [vmem] * 9,
        out_specs=(vmem, vmem),
        scratch_shapes=[
            pltpu.VMEM((n, 2 * rows, cols), F32),
            pltpu.VMEM((n, cols), F32),
            pltpu.VMEM((3, TALL, cols), F32),
        ],
        compiler_params=small,
    )(thickness, both, beyond, both1, beyond1, kept, temp, u, v, levels)
    return temp_gradient.reshape(count, rows, cols), surface_gradient


def solution(mesh):
    return jax.shard_map(
        on_device,
        mesh=mesh,
        in_specs=(
            P("grp", "ja", "ia"),
            P(("grp", "ja"), "ia"),
            P(None, None, "ja", "ia"),
            P(None, None, "ja", "ia"),
            P("ja", "ia"),
            P("ia"),
            P(),
            P(),
        ),
        out_specs=(P("grp", "ja", "ia"), P(("grp", "ja"), "ia")),
        check_vma=False,
    )
```

```python
import jax
import jax.numpy as jnp
from jax import lax
from jax.experimental import pallas as pl
from jax.experimental.pallas import tpu as pltpu
from jax.sharding import PartitionSpec as P

SOLVER_ITERS = 2
SURFACE_COEF = 2.0
F32 = jnp.float32

EDGE1, PART1, LEV1, ROWS1 = 16, 32, 33, 40
EDGE2, HROW2, LINE2, FLUX2, ROWS2 = 16, 24, 25, 50, 64
PEER1, PEER2 = 104, 32
WINDOW = 16
TALL = 32


def iota(shape, dim):
    return lax.broadcasted_iota(jnp.int32, shape, dim)


def full_sum(x):
    return jnp.sum(jnp.sum(x, axis=0), axis=(0, 1), keepdims=True)


def split_index(column, cols):
    return column >> (cols.bit_length() - 1), column & (cols - 1)


def fold_take(values, block, lane):
    out = jnp.zeros(block.shape, F32)
    for b in range(values.shape[0]):
        source = jnp.broadcast_to(values[b : b + 1], block.shape)
        out = jnp.where(block == b, jnp.take_along_axis(source, lane, axis=1), out)
    return out


def shift_blocks(x, step):
    return jnp.concatenate([x[step:], x[:step]], axis=0)


def surface_apply(field, block, lane):
    n, rows, cols = field.shape
    col = iota(field.shape, 2)
    row = iota(field.shape, 1)
    left = pltpu.roll(field, 1, 2)
    right = pltpu.roll(field, cols - 1, 2)
    west = jnp.where(col == 0, shift_blocks(left, n - 1), left)
    east = jnp.where(col == cols - 1, shift_blocks(right, 1), right)
    across = fold_take(field[:, rows - 1, :], block, lane)
    north = jnp.where(row == rows - 1, across[:, None, :], pltpu.roll(field, rows - 1, 1))
    south = jnp.where(row == 0, 0.0, pltpu.roll(field, 1, 1))
    return (1.0 + 4.0 * SURFACE_COEF) * field - SURFACE_COEF * (east + west + north + south)


def surface_solve(forcing, block, lane):
    residual = forcing
    direction = forcing
    iterate = None
    norm_now = full_sum(residual * residual)
    for sweep in range(SOLVER_ITERS):
        applied = surface_apply(direction, block, lane)
        step_size = norm_now / full_sum(direction * applied)
        part = step_size * direction
        iterate = part if iterate is None else iterate + part
        if sweep + 1 < SOLVER_ITERS:
            residual = residual - step_size * applied
            norm_next = full_sum(residual * residual)
            direction = residual + norm_next / norm_now * direction
            norm_now = norm_next
    return iterate


def level_rows(ref, base, count, rows):
    return ref[pl.ds(base, count, stride=rows), :]


def start_all(pairs, sems):
    copies = [pltpu.make_async_copy(src, dst, sems.at[i]) for i, (src, dst) in enumerate(pairs)]
    for copy in copies:
        copy.start()
    return copies


def pack_kernel(
    cp_in, th_in, adj_in, surf_in, u_in, v_in, lev_in, par_in, out, peer, depth_out, cp_out, th_out,
    cp, adj, surf, u, v, lev, par, sems
):
    copies = start_all(
        ((cp_in, cp), (lev_in, lev), (surf_in, surf), (par_in, par), (adj_in, adj), (u_in, u), (v_in, v), (cp_in, cp_out), (th_in, th_out)),
        sems,
    )
    for copy in copies[:5]:
        copy.wait()
    rows, cols = surf.shape
    count = adj.shape[0] // rows
    top = lax.axis_index("ja") == lax.axis_size("ja") - 1
    lane = iota((rows, cols), 1)
    depth = lev[...].astype(F32)
    depth_out[...] = depth
    forcing = surf[...]
    last = cols - 1
    edge = jnp.where(lane == 4 * count, depth[:, last:], 0.0)
    edge = jnp.where(lane == 4 * count + 1, depth[:, :1], edge)
    for k in range(count):
        here = adj[k * rows : (k + 1) * rows, :]
        forcing = forcing + cp[k] * jnp.where(depth > k, here, 0.0)
        edge = jnp.where(lane == k, here[:, last:], edge)
        edge = jnp.where(lane == 3 * count + k, here[:, :1], edge)
    copies[5].wait()
    for k in range(count):
        u0 = u[0, k * rows : (k + 1) * rows, :]
        u1 = u[1, k * rows : (k + 1) * rows, :]
        edge = jnp.where(lane == count + k, u1[:, last:], edge)
        edge = jnp.where(lane == 2 * count + k, u0[:, last:], edge)
    for copy in copies[6:]:
        copy.wait()
    out[0:rows, :] = forcing
    out[EDGE1 : EDGE1 + rows, :] = edge
    out[PART1:ROWS1, :] = jnp.zeros((ROWS1 - PART1, cols), F32)
    out[PART1 : PART1 + 1, :] = par[...].astype(F32)
    out[LEV1 : LEV1 + 1, :] = depth[rows - 1 :]
    peer[...] = jnp.zeros(peer.shape, F32)
    is_top = jnp.full((count, cols), top.astype(jnp.int32)) == 1
    last_row = level_rows(adj, rows - 1, count, rows)
    peer[0:count, :] = jnp.where(is_top, level_rows(adj, 0, count, rows), last_row)
    peer[count : 2 * count, :] = v[1, pl.ds(rows - 1, count, stride=rows), :]
    peer[2 * count : 3 * count, :] = v[0, pl.ds(rows - 1, count, stride=rows), :]
    peer[3 * count : 4 * count, :] = last_row
    peer[4 * count : 4 * count + 1, :] = jnp.where(is_top[:1], depth[:1], depth[rows - 1 :])


def parity(x):
    for shift in (8, 4, 2, 1):
        x = x ^ (x >> shift)
    return x & 1


def exchange_steps(n, kind):
    steps = []
    while n > 1:
        n //= 2
        steps.append(n)
    return steps if kind == 0 else steps[:1] + steps[:0:-1]


def slot_of(distance, n, kind):
    out = 0
    for r, step in enumerate(exchange_steps(n, kind)):
        out = out | (((distance >> (step.bit_length() - 1)) & 1) << r)
    return out


class Messages:
    def __init__(self, both):
        self.both = both
        self.count = both.shape[1]
        self.me = lax.axis_index("ia")
        self.kind = parity(self.me) ^ lax.axis_index("ja")
        self.own = [slot_of(self.me, self.count, kind) for kind in range(2)]

    def part(self, block, core, start, stop):
        kind = parity(block) ^ core
        slot = self.own[kind] ^ slot_of(block, self.count, kind)
        return self.both[self.kind ^ kind, slot, start:stop, :]

    def beside(self, block, start, stop):
        kind = parity(block) ^ lax.axis_index("ja")
        away = block ^ self.me
        slot = jnp.where(
            kind == 0, slot_of(away, self.count, 0), slot_of(away, self.count, 1)
        )
        return self.both[self.kind ^ kind, slot, start:stop, :]

    def field(self, rows):
        blocks = [
            jnp.concatenate([self.part(b, 0, 0, rows), self.part(b, 1, 0, rows)], axis=0)
            for b in range(self.count)
        ]
        return jnp.stack(blocks, axis=0)

    def line(self, core, index, out):
        for b in range(self.count):
            out[b : b + 1, :] = self.part(b, core, index, index + 1)
        return out[...]


def level_column(values, count, cols):
    level = iota((TALL, cols), 0)
    out = jnp.zeros((TALL, cols), F32)
    for k in range(count):
        out = jnp.where(level == k, values[k], out)
    return out


def position(n):
    me = lax.axis_index("ia")
    return me, lax.rem(me + n - 1, n), lax.rem(me + 1, n)


def sweep_levels(count, rows, th, fetch, west_of, east_of, u, v, pieces, top, depth, masks, emit):
    own, left, right, beside, beside_temp, beside_v = pieces
    east_depth, west_depth, north_depth, south_depth = masks
    cols = own.shape[1]
    lane = iota((rows, cols), 1)
    row = iota((rows, cols), 0)
    is_top = jnp.full((1, cols), top.astype(jnp.int32)) == 1
    for k in range(count):
        here = fetch(k)
        add = th[k] * own
        mid = here + jnp.where(depth > k, add, 0.0)
        bare = here + add
        u_west, t_west = west_of(k)
        west_value = t_west + th[k] * left
        east_value = jnp.where(
            lane == cols - 1, east_of(k) + th[k] * right, pltpu.roll(bare, cols - 1, 1)
        )
        u_here = u[k * rows : (k + 1) * rows, :]
        v_here = v[k * rows : (k + 1) * rows, :]
        flux_east = jnp.where(east_depth > k, 0.25 * u_here * (east_value - bare), 0.0)
        flux_first = jnp.where(west_depth > k, 0.25 * u_west * (bare - west_value), 0.0)
        flux_west = jnp.where(lane == 0, flux_first, pltpu.roll(flux_east, 1, 1))
        beside_value = beside_temp(k) + th[k] * beside
        above = jnp.where(is_top, 0.0, beside_value)
        north_value = jnp.where(row == rows - 1, above, pltpu.roll(bare, rows - 1, 0))
        flux_north = jnp.where(north_depth > k, 0.25 * v_here * (north_value - bare), 0.0)
        flux_below = jnp.where(south_depth > k, 0.25 * beside_v(k) * (bare[:1] - beside_value), 0.0)
        flux_south = jnp.where(row == 0, flux_below, pltpu.roll(flux_north, 1, 0))
        emit(k, mid + flux_east + flux_west + flux_north + flux_south)


def face_depths(depth, edge_left, edge_right, beside_depth, count, top):
    rows, cols = depth.shape
    lane = iota(depth.shape, 1)
    row = iota(depth.shape, 0)
    is_top = jnp.full(depth.shape, top.astype(jnp.int32)) == 1
    right = edge_right[:, 4 * count + 1 : 4 * count + 2]
    east = jnp.minimum(depth, jnp.where(lane == cols - 1, right, pltpu.roll(depth, cols - 1, 1)))
    west = jnp.minimum(depth, edge_left[:, 4 * count : 4 * count + 1])
    above = jnp.where(is_top, depth, beside_depth)
    north = jnp.minimum(depth, jnp.where(row == rows - 1, above, pltpu.roll(depth, rows - 1, 0)))
    south = jnp.where(is_top[:1], jnp.minimum(depth[:1], beside_depth), 0.0)
    return east, west, north, south


def load_pieces(solved, me, west, east, rows, top):
    cols = solved.shape[-1]
    here = pl.ds(pl.multiple_of(jnp.where(top, rows, 0), 8), rows)
    own = solved[me, here, :]
    left = pltpu.roll(solved[west, here, :], 1, 1)
    right = pltpu.roll(solved[east, here, :], cols - 1, 1)
    is_top = jnp.full((1, cols), top.astype(jnp.int32)) == 1
    block = solved[me]
    beside = jnp.where(is_top, block[rows - 1 : rows], block[rows : rows + 1])
    return own, left, right, beside


def first_kernel(
    cp, th, both, beyond, adj, u_in, v_in, depth_in, t_out, out, peer, kept, solved, rowbuf, tall
):
    u, v = u_in.at[1], v_in.at[1]
    rows, cols = depth_in.shape
    count = adj.shape[0] // rows
    top = lax.axis_index("ja") == lax.axis_size("ja") - 1
    sent = Messages(both)
    me, west, east = position(sent.count)
    partner = sent.line(0, PART1, rowbuf).astype(jnp.int32)
    block, lane = split_index(partner, cols)
    solved[...] = surface_solve(sent.field(rows), block, lane)
    depths = sent.line(1, LEV1, rowbuf)
    fold_depth = rowbuf[pl.ds(me, 1), :]
    rowbuf[...] = fold_take(depths, block, lane)
    across_depth = rowbuf[pl.ds(me, 1), :]

    is_top = jnp.full((count, cols), top.astype(jnp.int32)) == 1
    level = iota((TALL, cols), 0).astype(F32)
    tall[0, 0:count, :] = jnp.where(
        is_top, level_rows(v, rows - 1, count, rows), beyond[count : 2 * count, :]
    )
    tall[1, 0:count, :] = jnp.where(
        is_top, level_rows(adj, rows - 1, count, rows), beyond[3 * count : 4 * count, :]
    )
    fold_solved = solved[me, 2 * rows - 8 :, :][7:]
    flux = jnp.where(
        fold_depth > level,
        0.25 * tall[0] * (tall[1] + level_column(th, count, cols) * fold_solved),
        0.0,
    )
    into = jnp.where(across_depth > level, level_column(cp, count, cols) * flux, 0.0)
    kept[0:TALL, :] = flux
    kept[TALL:, :] = jnp.broadcast_to(across_depth, (8, cols))
    out[HROW2 : HROW2 + 1, :] = jnp.sum(into, axis=0, keepdims=True)

    depth = depth_in[...]
    edge_left = sent.beside(west, EDGE1, EDGE1 + rows)
    edge_right = sent.beside(east, EDGE1, EDGE1 + rows)
    beside_depth = beyond[4 * count : 4 * count + 1, :]
    masks = face_depths(depth, edge_left, edge_right, beside_depth, count, top)
    own, left, right, beside = load_pieces(solved, me, west, east, rows, top)
    pieces = (
        own,
        left,
        right,
        beside,
        lambda k: beyond[k : k + 1, :],
        lambda k: beyond[count + k : count + k + 1, :],
    )
    spot = iota((rows, cols), 1)
    carry = {"forcing": own, "edge": jnp.zeros((rows, cols), F32)}

    def emit(k, value):
        t_out[k * rows : (k + 1) * rows, :] = value
        carry["forcing"] = carry["forcing"] + cp[k] * jnp.where(depth > k, value, 0.0)
        edge = jnp.where(spot == k, value[:, cols - 1 :], carry["edge"])
        carry["edge"] = jnp.where(spot == count + k, value[:, :1], edge)

    sweep_levels(
        count,
        rows,
        th,
        lambda k: adj[k * rows : (k + 1) * rows, :],
        lambda k: (edge_left[:, count + k : count + k + 1], edge_left[:, k : k + 1]),
        lambda k: edge_right[:, 3 * count + k : 3 * count + k + 1],
        u,
        v,
        pieces,
        top,
        depth,
        masks,
        emit,
    )
    out[0:rows, :] = carry["forcing"]
    half = rows // 2
    edge = carry["edge"]
    out[EDGE2 : EDGE2 + half, :] = jnp.where(
        spot[:half] < cols // 2, edge[:half], pltpu.roll(edge[half:], cols // 2, 1)
    )
    last_row = level_rows(t_out, rows - 1, count, rows)
    out[LINE2 : LINE2 + count, :] = jnp.where(is_top, last_row, beyond[2 * count : 3 * count, :])
    later, share = count // 2, count - count // 2
    out[FLUX2 : FLUX2 + share, :] = jnp.where(
        is_top[:share], kept[later:count, :], kept[0:share, :]
    )
    out[FLUX2 + share :, :] = jnp.zeros((ROWS2 - FLUX2 - share, cols), F32)
    peer[0:count, :] = jnp.where(is_top, level_rows(t_out, 0, count, rows), last_row)
    peer[count:, :] = jnp.zeros((peer.shape[0] - count, cols), F32)


def second_kernel(
    th, both, beyond, both1, beyond1, kept, temp, u_in, v_in, depth_in, t_out, s_out, solved, rowbuf, tall
):
    u, v = u_in.at[0], v_in.at[0]
    rows, cols = depth_in.shape
    count = temp.shape[0] // rows
    top = lax.axis_index("ja") == lax.axis_size("ja") - 1
    sent, sent1 = Messages(both), Messages(both1)
    n = sent.count
    me, west, east = position(n)
    partners = sent1.line(0, PART1, rowbuf)
    partner = partners.astype(jnp.int32)
    block, lane = split_index(partner, cols)
    forcing = sent.field(rows)
    fold = fold_take(sent.line(0, HROW2, rowbuf), block, lane)
    row3 = iota(forcing.shape, 1)
    forcing = forcing - jnp.where(row3 == 2 * rows - 1, fold[:, None, :], 0.0)
    iterate = surface_solve(forcing, block, lane)
    solved[...] = iterate
    rowbuf[...] = fold_take(iterate[:, 2 * rows - 1, :], block, lane)
    across_solved = rowbuf[pl.ds(me, 1), :]

    spot = iota((1, cols), 1)
    rowbuf[...] = partners
    beside_left = pltpu.roll(rowbuf[pl.ds(west, 1), :], 1, 1)
    beside_right = pltpu.roll(rowbuf[pl.ds(east, 1), :], cols - 1, 1)
    end_partner = jnp.where(spot == 0, beside_left, beside_right)
    end_partner = jnp.where((spot == 0) | (spot == cols - 1), end_partner, 0.0)
    own_partner = jnp.broadcast_to(rowbuf[pl.ds(me, 1), :], (TALL, cols)).astype(jnp.int32)
    end_partner = jnp.broadcast_to(end_partner, (WINDOW, cols)).astype(jnp.int32)
    own_block, own_lane = split_index(own_partner, cols)
    end_block, end_lane = split_index(end_partner, cols)
    zero, low = jnp.zeros((TALL, cols), F32), jnp.zeros((WINDOW, cols), F32)
    temp_across, v_across = zero, zero
    own_flux, end_flux = [low, low], [low, low]
    for b in range(n):
        here, there = own_block == b, end_block == b
        line = sent.part(b, 1, LINE2, LINE2 + TALL)
        temp_across = jnp.where(here, jnp.take_along_axis(line, own_lane, axis=1), temp_across)
        line = sent.part(b, 0, LINE2, LINE2 + TALL)
        v_across = jnp.where(here, jnp.take_along_axis(line, own_lane, axis=1), v_across)
        for c in range(2):
            line = sent.part(b, c, ROWS2 - WINDOW, ROWS2)
            moved = jnp.take_along_axis(line, own_lane[:WINDOW], axis=1)
            own_flux[c] = jnp.where(here[:WINDOW], moved, own_flux[c])
            moved = jnp.take_along_axis(line, end_lane, axis=1)
            end_flux[c] = jnp.where(there, moved, end_flux[c])
    skip = FLUX2 - (ROWS2 - WINDOW)
    later, share = count // 2, count - count // 2
    for i, parts in enumerate((own_flux, end_flux)):
        for c, start in ((0, 0), (1, later)):
            tall[2, 0:WINDOW, :] = parts[c]
            tall[i, start : start + share, :] = tall[2, skip : skip + share, :]
    level = iota((TALL, cols), 0).astype(F32)
    fold_last = jnp.where(
        kept[TALL : TALL + 1, :] > level,
        0.25
        * v_across
        * (temp_across - kept[0:TALL, :] + level_column(th, count, cols) * across_solved),
        0.0,
    )
    tall[2] = fold_last

    depth = depth_in[...]
    edge1_left = sent1.beside(west, EDGE1, EDGE1 + rows)
    edge1_right = sent1.beside(east, EDGE1, EDGE1 + rows)
    half = rows // 2

    def both_rows(line):
        return jnp.concatenate([line, pltpu.roll(line, cols // 2, 1)], axis=0)

    edge_left = both_rows(sent.beside(west, EDGE2, EDGE2 + half))
    edge_right = both_rows(sent.beside(east, EDGE2, EDGE2 + half))
    beside_depth = beyond1[4 * count : 4 * count + 1, :]
    masks = face_depths(depth, edge1_left, edge1_right, beside_depth, count, top)
    own, left, right, beside = load_pieces(solved, me, west, east, rows, top)
    s_out[...] = own
    pieces = (
        own,
        left,
        right,
        beside,
        lambda k: beyond[k : k + 1, :],
        lambda k: beyond1[2 * count + k : 2 * count + k + 1, :],
    )
    row = iota((rows, cols), 0)
    on_fold = (row == rows - 1) & (jnp.full((rows, cols), top.astype(jnp.int32)) == 1)

    def less(value, index, k):
        return value - jnp.where(on_fold, tall[index, k : k + 1, :], 0.0)

    def emit(k, value):
        t_out[k * rows : (k + 1) * rows, :] = less(value, 2, k)

    def spread(column):
        return jnp.broadcast_to(column, (rows, cols))

    sweep_levels(
        count,
        rows,
        th,
        lambda k: less(temp[k * rows : (k + 1) * rows, :], 0, k),
        lambda k: (
            edge1_left[:, 2 * count + k : 2 * count + k + 1],
            less(spread(edge_left[:, k : k + 1]), 1, k),
        ),
        lambda k: less(spread(edge_right[:, count + k : count + k + 1]), 1, k),
        u,
        v,
        pieces,
        top,
        depth,
        masks,
        emit,
    )


def exchange(block, peer):
    n = lax.axis_size("ia")
    rows, cols = block.shape
    kinds = [exchange_steps(n, kind) for kind in range(2)]
    y = block
    for near, far in zip(*kinds):
        pairs = []
        for i in range(n):
            for c in range(2):
                step = far if parity(i) ^ c else near
                pairs.append((2 * i + c, 2 * (i ^ step) + 1 - c))
        y = jnp.concatenate([y, lax.ppermute(y, ("ia", "ja"), pairs)])
    z = lax.ppermute(jnp.concatenate([y, peer]), "ja", [(0, 1), (1, 0)])
    both = jnp.concatenate([y, z[: n * rows]]).reshape(2, n, rows, cols)
    return both, z[n * rows :]


def on_device(
    adjoint_temp, adjoint_surface, trajectory_u, trajectory_v, levels, partner, thickness, coupling
):
    steps, count, rows, cols = trajectory_u.shape
    n = lax.axis_size("ia")
    flat = count * rows
    adj = adjoint_temp.reshape(flat, cols)
    u = trajectory_u.reshape(steps, flat, cols)
    v = trajectory_v.reshape(steps, flat, cols)
    par = partner.reshape(1, cols)

    def stay(x):
        return pltpu.with_memory_space_constraint(x, pltpu.HBM)

    smem = pl.BlockSpec(memory_space=pltpu.SMEM)
    vmem = pl.BlockSpec(memory_space=pltpu.VMEM)
    hbm = pl.BlockSpec(memory_space=pltpu.HBM)

    def shape(*dims):
        return jax.ShapeDtypeStruct(dims, F32)

    small = pltpu.CompilerParams(vmem_limit_bytes=(8 + n // 2) * 2**20)
    out, peer, depth, cp, th = pl.pallas_call(
        pack_kernel,
        out_shape=(
            shape(ROWS1, cols),
            shape(PEER1, cols),
            shape(rows, cols),
            shape(count),
            shape(count),
        ),
        in_specs=[hbm] * 8,
        out_specs=(vmem,) * 5,
        scratch_shapes=[
            pltpu.SMEM((count,), F32),
            pltpu.VMEM((flat, cols), F32),
            pltpu.VMEM((rows, cols), F32),
            pltpu.VMEM((steps, flat, cols), F32),
            pltpu.VMEM((steps, flat, cols), F32),
            pltpu.VMEM((rows, cols), jnp.int32),
            pltpu.VMEM((1, cols), jnp.int32),
            pltpu.SemaphoreType.DMA((9,)),
        ],
        compiler_params=small,
    )(*(stay(x) for x in (coupling, thickness, adj, adjoint_surface, u, v, levels, par)))
    both1, beyond1 = exchange(out, peer)
    temp, out, peer, kept = pl.pallas_call(
        first_kernel,
        out_shape=(
            shape(flat, cols),
            shape(ROWS2, cols),
            shape(PEER2, cols),
            shape(TALL + 8, cols),
        ),
        in_specs=[smem, smem, vmem, vmem, vmem, vmem, vmem, vmem],
        out_specs=(vmem,) * 4,
        scratch_shapes=[
            pltpu.VMEM((n, 2 * rows, cols), F32),
            pltpu.VMEM((n, cols), F32),
            pltpu.VMEM((2, TALL, cols), F32),
        ],
        compiler_params=small,
    )(cp, th, both1, beyond1, adj, u, v, depth)
    both, beyond = exchange(out, peer)
    temp_gradient, surface_gradient = pl.pallas_call(
        second_kernel,
        out_shape=(shape(flat, cols), shape(rows, cols)),
        in_specs=[smem] + [vmem] * 6 + [vmem]*3,
        out_specs=(vmem, vmem),
        scratch_shapes=[
            pltpu.VMEM((n, 2 * rows, cols), F32),
            pltpu.VMEM((n, cols), F32),
            pltpu.VMEM((3, TALL, cols), F32),
        ],
        compiler_params=small,
    )(th, both, beyond, both1, beyond1, kept, temp, u, v, depth)
    return temp_gradient.reshape(count, rows, cols), surface_gradient


def solution(mesh):
    return jax.shard_map(
        on_device,
        mesh=mesh,
        in_specs=(
            P("grp", "ja", "ia"),
            P(("grp", "ja"), "ia"),
            P(None, None, "ja", "ia"),
            P(None, None, "ja", "ia"),
            P("ja", "ia"),
            P("ia"),
            P(),
            P(),
        ),
        out_specs=(P("grp", "ja", "ia"), P(("grp", "ja"), "ia")),
        check_vma=False,
    )
```

```python
import jax
import jax.numpy as jnp
from jax import lax
from jax.experimental import pallas as pl
from jax.experimental.pallas import tpu as pltpu
from jax.sharding import PartitionSpec as P

SOLVER_ITERS = 2
SURFACE_COEF = 2.0
F32 = jnp.float32

EDGE1, PART1, LEV1, ROWS1 = 16, 32, 33, 40
EDGE2, HROW2, LINE2, FLUX2, ROWS2 = 16, 24, 25, 50, 64
PEER1, PEER2 = 104, 32
WINDOW = 16
TALL = 32


def iota(shape, dim):
    return lax.broadcasted_iota(jnp.int32, shape, dim)


def full_sum(x):
    return jnp.sum(jnp.sum(x, axis=0), axis=(0, 1), keepdims=True)


def split_index(column, cols):
    return column >> (cols.bit_length() - 1), column & (cols - 1)


def fold_take(values, block, lane):
    out = jnp.zeros(block.shape, F32)
    for b in range(values.shape[0]):
        source = jnp.broadcast_to(values[b : b + 1], block.shape)
        out = jnp.where(block == b, jnp.take_along_axis(source, lane, axis=1), out)
    return out


def shift_blocks(x, step):
    return jnp.concatenate([x[step:], x[:step]], axis=0)


def surface_apply(field, block, lane):
    n, rows, cols = field.shape
    col = iota(field.shape, 2)
    row = iota(field.shape, 1)
    left = pltpu.roll(field, 1, 2)
    right = pltpu.roll(field, cols - 1, 2)
    west = jnp.where(col == 0, shift_blocks(left, n - 1), left)
    east = jnp.where(col == cols - 1, shift_blocks(right, 1), right)
    across = fold_take(field[:, rows - 1, :], block, lane)
    north = jnp.where(row == rows - 1, across[:, None, :], pltpu.roll(field, rows - 1, 1))
    south = jnp.where(row == 0, 0.0, pltpu.roll(field, 1, 1))
    return (1.0 + 4.0 * SURFACE_COEF) * field - SURFACE_COEF * (east + west + north + south)


def surface_solve(forcing, block, lane):
    residual = forcing
    direction = forcing
    iterate = None
    norm_now = full_sum(residual * residual)
    for sweep in range(SOLVER_ITERS):
        applied = surface_apply(direction, block, lane)
        step_size = norm_now / full_sum(direction * applied)
        part = step_size * direction
        iterate = part if iterate is None else iterate + part
        if sweep + 1 < SOLVER_ITERS:
            residual = residual - step_size * applied
            norm_next = full_sum(residual * residual)
            direction = residual + norm_next / norm_now * direction
            norm_now = norm_next
    return iterate


def level_rows(ref, base, count, rows):
    return ref[pl.ds(base, count, stride=rows), :]


def start_all(pairs, sems):
    copies = [pltpu.make_async_copy(src, dst, sems.at[i]) for i, (src, dst) in enumerate(pairs)]
    for copy in copies:
        copy.start()
    return copies


def pack_kernel(
    cp_in, th_in, adj_in, surf_in, u_in, v_in, lev_in, par_in, out, peer, depth_out, cp_out, th_out,
    cp, th, adj, surf, u, v, lev, par, sems
):
    copies = start_all(
        ((cp_in, cp), (lev_in, lev), (surf_in, surf), (par_in, par), (adj_in, adj), (u_in, u), (v_in, v), (th_in, th)),
        sems,
    )
    for copy in copies[:5]:
        copy.wait()
    rows, cols = surf.shape
    count = adj.shape[0] // rows
    top = lax.axis_index("ja") == lax.axis_size("ja") - 1
    lane = iota((rows, cols), 1)
    depth = lev[...].astype(F32)
    depth_out[...] = depth
    forcing = surf[...]
    last = cols - 1
    edge = jnp.where(lane == 4 * count, depth[:, last:], 0.0)
    edge = jnp.where(lane == 4 * count + 1, depth[:, :1], edge)
    for k in range(count):
        here = adj[k * rows : (k + 1) * rows, :]
        forcing = forcing + cp[k] * jnp.where(depth > k, here, 0.0)
        edge = jnp.where(lane == k, here[:, last:], edge)
        edge = jnp.where(lane == 3 * count + k, here[:, :1], edge)
    copies[5].wait()
    for k in range(count):
        u0 = u[0, k * rows : (k + 1) * rows, :]
        u1 = u[1, k * rows : (k + 1) * rows, :]
        edge = jnp.where(lane == count + k, u1[:, last:], edge)
        edge = jnp.where(lane == 2 * count + k, u0[:, last:], edge)
    for copy in copies[6:]:
        copy.wait()
    cp_out[...] = level_column(cp, count, cols)
    th_out[...] = level_column(th, count, cols)
    out[0:rows, :] = forcing
    out[EDGE1 : EDGE1 + rows, :] = edge
    out[PART1:ROWS1, :] = jnp.zeros((ROWS1 - PART1, cols), F32)
    out[PART1 : PART1 + 1, :] = par[...].astype(F32)
    out[LEV1 : LEV1 + 1, :] = depth[rows - 1 :]
    peer[...] = jnp.zeros(peer.shape, F32)
    is_top = jnp.full((count, cols), top.astype(jnp.int32)) == 1
    last_row = level_rows(adj, rows - 1, count, rows)
    peer[0:count, :] = jnp.where(is_top, level_rows(adj, 0, count, rows), last_row)
    peer[count : 2 * count, :] = v[1, pl.ds(rows - 1, count, stride=rows), :]
    peer[2 * count : 3 * count, :] = v[0, pl.ds(rows - 1, count, stride=rows), :]
    peer[3 * count : 4 * count, :] = last_row
    peer[4 * count : 4 * count + 1, :] = jnp.where(is_top[:1], depth[:1], depth[rows - 1 :])


def parity(x):
    for shift in (8, 4, 2, 1):
        x = x ^ (x >> shift)
    return x & 1


def exchange_steps(n, kind):
    steps = []
    while n > 1:
        n //= 2
        steps.append(n)
    return steps if kind == 0 else steps[:1] + steps[:0:-1]


def slot_of(distance, n, kind):
    out = 0
    for r, step in enumerate(exchange_steps(n, kind)):
        out = out | (((distance >> (step.bit_length() - 1)) & 1) << r)
    return out


class Messages:
    def __init__(self, both):
        self.both = both
        self.count = both.shape[1]
        self.me = lax.axis_index("ia")
        self.kind = parity(self.me) ^ lax.axis_index("ja")
        self.own = [slot_of(self.me, self.count, kind) for kind in range(2)]

    def part(self, block, core, start, stop):
        kind = parity(block) ^ core
        slot = self.own[kind] ^ slot_of(block, self.count, kind)
        return self.both[self.kind ^ kind, slot, start:stop, :]

    def beside(self, block, start, stop):
        kind = parity(block) ^ lax.axis_index("ja")
        away = block ^ self.me
        slot = jnp.where(
            kind == 0, slot_of(away, self.count, 0), slot_of(away, self.count, 1)
        )
        return self.both[self.kind ^ kind, slot, start:stop, :]

    def field(self, rows):
        blocks = [
            jnp.concatenate([self.part(b, 0, 0, rows), self.part(b, 1, 0, rows)], axis=0)
            for b in range(self.count)
        ]
        return jnp.stack(blocks, axis=0)

    def line(self, core, index, out):
        for b in range(self.count):
            out[b : b + 1, :] = self.part(b, core, index, index + 1)
        return out[...]


def level_column(values, count, cols):
    level = iota((TALL, cols), 0)
    out = jnp.zeros((TALL, cols), F32)
    for k in range(count):
        out = jnp.where(level == k, values[k], out)
    return out


def position(n):
    me = lax.axis_index("ia")
    return me, lax.rem(me + n - 1, n), lax.rem(me + 1, n)


def sweep_levels(count, rows, th, fetch, west_of, east_of, u, v, pieces, top, depth, masks, emit):
    own, left, right, beside, beside_temp, beside_v = pieces
    east_depth, west_depth, north_depth, south_depth = masks
    cols = own.shape[1]
    lane = iota((rows, cols), 1)
    row = iota((rows, cols), 0)
    is_top = jnp.full((1, cols), top.astype(jnp.int32)) == 1
    for k in range(count):
        here = fetch(k)
        weight = th[k : k + 1, :]
        add = weight * own
        mid = here + jnp.where(depth > k, add, 0.0)
        bare = here + add
        u_west, t_west = west_of(k)
        west_value = t_west + weight * left
        east_value = jnp.where(
            lane == cols - 1, east_of(k) + weight * right, pltpu.roll(bare, cols - 1, 1)
        )
        u_here = u[k * rows : (k + 1) * rows, :]
        v_here = v[k * rows : (k + 1) * rows, :]
        flux_east = jnp.where(east_depth > k, 0.25 * u_here * (east_value - bare), 0.0)
        flux_first = jnp.where(west_depth > k, 0.25 * u_west * (bare - west_value), 0.0)
        flux_west = jnp.where(lane == 0, flux_first, pltpu.roll(flux_east, 1, 1))
        beside_value = beside_temp(k) + weight * beside
        above = jnp.where(is_top, 0.0, beside_value)
        north_value = jnp.where(row == rows - 1, above, pltpu.roll(bare, rows - 1, 0))
        flux_north = jnp.where(north_depth > k, 0.25 * v_here * (north_value - bare), 0.0)
        flux_below = jnp.where(south_depth > k, 0.25 * beside_v(k) * (bare[:1] - beside_value), 0.0)
        flux_south = jnp.where(row == 0, flux_below, pltpu.roll(flux_north, 1, 0))
        emit(k, mid + flux_east + flux_west + flux_north + flux_south)


def face_depths(depth, edge_left, edge_right, beside_depth, count, top):
    rows, cols = depth.shape
    lane = iota(depth.shape, 1)
    row = iota(depth.shape, 0)
    is_top = jnp.full(depth.shape, top.astype(jnp.int32)) == 1
    right = edge_right[:, 4 * count + 1 : 4 * count + 2]
    east = jnp.minimum(depth, jnp.where(lane == cols - 1, right, pltpu.roll(depth, cols - 1, 1)))
    west = jnp.minimum(depth, edge_left[:, 4 * count : 4 * count + 1])
    above = jnp.where(is_top, depth, beside_depth)
    north = jnp.minimum(depth, jnp.where(row == rows - 1, above, pltpu.roll(depth, rows - 1, 0)))
    south = jnp.where(is_top[:1], jnp.minimum(depth[:1], beside_depth), 0.0)
    return east, west, north, south


def load_pieces(solved, me, west, east, rows, top):
    cols = solved.shape[-1]
    here = pl.ds(pl.multiple_of(jnp.where(top, rows, 0), 8), rows)
    own = solved[me, here, :]
    left = pltpu.roll(solved[west, here, :], 1, 1)
    right = pltpu.roll(solved[east, here, :], cols - 1, 1)
    is_top = jnp.full((1, cols), top.astype(jnp.int32)) == 1
    block = solved[me]
    beside = jnp.where(is_top, block[rows - 1 : rows], block[rows : rows + 1])
    return own, left, right, beside


def first_kernel(
    cp, th, both, beyond, adj, u_in, v_in, depth_in, t_out, out, peer, kept, solved, rowbuf, tall
):
    u, v = u_in.at[1], v_in.at[1]
    rows, cols = depth_in.shape
    count = adj.shape[0] // rows
    top = lax.axis_index("ja") == lax.axis_size("ja") - 1
    sent = Messages(both)
    me, west, east = position(sent.count)
    partner = sent.line(0, PART1, rowbuf).astype(jnp.int32)
    block, lane = split_index(partner, cols)
    solved[...] = surface_solve(sent.field(rows), block, lane)
    depths = sent.line(1, LEV1, rowbuf)
    fold_depth = rowbuf[pl.ds(me, 1), :]
    rowbuf[...] = fold_take(depths, block, lane)
    across_depth = rowbuf[pl.ds(me, 1), :]

    is_top = jnp.full((count, cols), top.astype(jnp.int32)) == 1
    level = iota((TALL, cols), 0).astype(F32)
    tall[0, 0:count, :] = jnp.where(
        is_top, level_rows(v, rows - 1, count, rows), beyond[count : 2 * count, :]
    )
    tall[1, 0:count, :] = jnp.where(
        is_top, level_rows(adj, rows - 1, count, rows), beyond[3 * count : 4 * count, :]
    )
    fold_solved = solved[me, 2 * rows - 8 :, :][7:]
    flux = jnp.where(
        fold_depth > level,
        0.25 * tall[0] * (tall[1] + th[...] * fold_solved),
        0.0,
    )
    into = jnp.where(across_depth > level, cp[...] * flux, 0.0)
    kept[0:TALL, :] = flux
    kept[TALL:, :] = jnp.broadcast_to(across_depth, (8, cols))
    out[HROW2 : HROW2 + 1, :] = jnp.sum(into, axis=0, keepdims=True)

    depth = depth_in[...]
    edge_left = sent.beside(west, EDGE1, EDGE1 + rows)
    edge_right = sent.beside(east, EDGE1, EDGE1 + rows)
    beside_depth = beyond[4 * count : 4 * count + 1, :]
    masks = face_depths(depth, edge_left, edge_right, beside_depth, count, top)
    own, left, right, beside = load_pieces(solved, me, west, east, rows, top)
    pieces = (
        own,
        left,
        right,
        beside,
        lambda k: beyond[k : k + 1, :],
        lambda k: beyond[count + k : count + k + 1, :],
    )
    spot = iota((rows, cols), 1)
    carry = {"forcing": own, "edge": jnp.zeros((rows, cols), F32)}

    def emit(k, value):
        t_out[k * rows : (k + 1) * rows, :] = value
        carry["forcing"] = carry["forcing"] + cp[k : k + 1, :] * jnp.where(depth > k, value, 0.0)
        edge = jnp.where(spot == k, value[:, cols - 1 :], carry["edge"])
        carry["edge"] = jnp.where(spot == count + k, value[:, :1], edge)

    sweep_levels(
        count,
        rows,
        th,
        lambda k: adj[k * rows : (k + 1) * rows, :],
        lambda k: (edge_left[:, count + k : count + k + 1], edge_left[:, k : k + 1]),
        lambda k: edge_right[:, 3 * count + k : 3 * count + k + 1],
        u,
        v,
        pieces,
        top,
        depth,
        masks,
        emit,
    )
    out[0:rows, :] = carry["forcing"]
    half = rows // 2
    edge = carry["edge"]
    out[EDGE2 : EDGE2 + half, :] = jnp.where(
        spot[:half] < cols // 2, edge[:half], pltpu.roll(edge[half:], cols // 2, 1)
    )
    last_row = level_rows(t_out, rows - 1, count, rows)
    out[LINE2 : LINE2 + count, :] = jnp.where(is_top, last_row, beyond[2 * count : 3 * count, :])
    later, share = count // 2, count - count // 2
    out[FLUX2 : FLUX2 + share, :] = jnp.where(
        is_top[:share], kept[later:count, :], kept[0:share, :]
    )
    out[FLUX2 + share :, :] = jnp.zeros((ROWS2 - FLUX2 - share, cols), F32)
    peer[0:count, :] = jnp.where(is_top, level_rows(t_out, 0, count, rows), last_row)
    peer[count:, :] = jnp.zeros((peer.shape[0] - count, cols), F32)


def second_kernel(
    th, both, beyond, both1, beyond1, kept, temp, u_in, v_in, depth_in, t_out, s_out, solved, rowbuf, tall
):
    u, v = u_in.at[0], v_in.at[0]
    rows, cols = depth_in.shape
    count = temp.shape[0] // rows
    top = lax.axis_index("ja") == lax.axis_size("ja") - 1
    sent, sent1 = Messages(both), Messages(both1)
    n = sent.count
    me, west, east = position(n)
    partners = sent1.line(0, PART1, rowbuf)
    partner = partners.astype(jnp.int32)
    block, lane = split_index(partner, cols)
    forcing = sent.field(rows)
    fold = fold_take(sent.line(0, HROW2, rowbuf), block, lane)
    row3 = iota(forcing.shape, 1)
    forcing = forcing - jnp.where(row3 == 2 * rows - 1, fold[:, None, :], 0.0)
    iterate = surface_solve(forcing, block, lane)
    solved[...] = iterate
    rowbuf[...] = fold_take(iterate[:, 2 * rows - 1, :], block, lane)
    across_solved = rowbuf[pl.ds(me, 1), :]

    spot = iota((1, cols), 1)
    rowbuf[...] = partners
    beside_left = pltpu.roll(rowbuf[pl.ds(west, 1), :], 1, 1)
    beside_right = pltpu.roll(rowbuf[pl.ds(east, 1), :], cols - 1, 1)
    end_partner = jnp.where(spot == 0, beside_left, beside_right)
    end_partner = jnp.where((spot == 0) | (spot == cols - 1), end_partner, 0.0)
    own_partner = jnp.broadcast_to(rowbuf[pl.ds(me, 1), :], (TALL, cols)).astype(jnp.int32)
    end_partner = jnp.broadcast_to(end_partner, (WINDOW, cols)).astype(jnp.int32)
    own_block, own_lane = split_index(own_partner, cols)
    end_block, end_lane = split_index(end_partner, cols)
    zero, low = jnp.zeros((TALL, cols), F32), jnp.zeros((WINDOW, cols), F32)
    temp_across, v_across = zero, zero
    own_flux, end_flux = [low, low], [low, low]
    for b in range(n):
        here, there = own_block == b, end_block == b
        line = sent.part(b, 1, LINE2, LINE2 + TALL)
        temp_across = jnp.where(here, jnp.take_along_axis(line, own_lane, axis=1), temp_across)
        line = sent.part(b, 0, LINE2, LINE2 + TALL)
        v_across = jnp.where(here, jnp.take_along_axis(line, own_lane, axis=1), v_across)
        for c in range(2):
            line = sent.part(b, c, ROWS2 - WINDOW, ROWS2)
            moved = jnp.take_along_axis(line, own_lane[:WINDOW], axis=1)
            own_flux[c] = jnp.where(here[:WINDOW], moved, own_flux[c])
            moved = jnp.take_along_axis(line, end_lane, axis=1)
            end_flux[c] = jnp.where(there, moved, end_flux[c])
    skip = FLUX2 - (ROWS2 - WINDOW)
    later, share = count // 2, count - count // 2
    for i, parts in enumerate((own_flux, end_flux)):
        for c, start in ((0, 0), (1, later)):
            tall[2, 0:WINDOW, :] = parts[c]
            tall[i, start : start + share, :] = tall[2, skip : skip + share, :]
    level = iota((TALL, cols), 0).astype(F32)
    fold_last = jnp.where(
        kept[TALL : TALL + 1, :] > level,
        0.25
        * v_across
        * (temp_across - kept[0:TALL, :] + th[...] * across_solved),
        0.0,
    )
    tall[2] = fold_last

    depth = depth_in[...]
    edge1_left = sent1.beside(west, EDGE1, EDGE1 + rows)
    edge1_right = sent1.beside(east, EDGE1, EDGE1 + rows)
    half = rows // 2

    def both_rows(line):
        return jnp.concatenate([line, pltpu.roll(line, cols // 2, 1)], axis=0)

    edge_left = both_rows(sent.beside(west, EDGE2, EDGE2 + half))
    edge_right = both_rows(sent.beside(east, EDGE2, EDGE2 + half))
    beside_depth = beyond1[4 * count : 4 * count + 1, :]
    masks = face_depths(depth, edge1_left, edge1_right, beside_depth, count, top)
    own, left, right, beside = load_pieces(solved, me, west, east, rows, top)
    s_out[...] = own
    pieces = (
        own,
        left,
        right,
        beside,
        lambda k: beyond[k : k + 1, :],
        lambda k: beyond1[2 * count + k : 2 * count + k + 1, :],
    )
    row = iota((rows, cols), 0)
    on_fold = (row == rows - 1) & (jnp.full((rows, cols), top.astype(jnp.int32)) == 1)

    def less(value, index, k):
        return value - jnp.where(on_fold, tall[index, k : k + 1, :], 0.0)

    def emit(k, value):
        t_out[k * rows : (k + 1) * rows, :] = less(value, 2, k)

    def spread(column):
        return jnp.broadcast_to(column, (rows, cols))

    sweep_levels(
        count,
        rows,
        th,
        lambda k: less(temp[k * rows : (k + 1) * rows, :], 0, k),
        lambda k: (
            edge1_left[:, 2 * count + k : 2 * count + k + 1],
            less(spread(edge_left[:, k : k + 1]), 1, k),
        ),
        lambda k: less(spread(edge_right[:, count + k : count + k + 1]), 1, k),
        u,
        v,
        pieces,
        top,
        depth,
        masks,
        emit,
    )


def exchange(block, peer):
    n = lax.axis_size("ia")
    rows, cols = block.shape
    kinds = [exchange_steps(n, kind) for kind in range(2)]
    y = block
    for near, far in zip(*kinds):
        pairs = []
        for i in range(n):
            for c in range(2):
                step = far if parity(i) ^ c else near
                pairs.append((2 * i + c, 2 * (i ^ step) + 1 - c))
        y = jnp.concatenate([y, lax.ppermute(y, ("ia", "ja"), pairs)])
    z = lax.ppermute(jnp.concatenate([y, peer]), "ja", [(0, 1), (1, 0)])
    both = jnp.concatenate([y, z[: n * rows]]).reshape(2, n, rows, cols)
    return both, z[n * rows :]


def on_device(
    adjoint_temp, adjoint_surface, trajectory_u, trajectory_v, levels, partner, thickness, coupling
):
    steps, count, rows, cols = trajectory_u.shape
    n = lax.axis_size("ia")
    flat = count * rows
    adj = adjoint_temp.reshape(flat, cols)
    u = trajectory_u.reshape(steps, flat, cols)
    v = trajectory_v.reshape(steps, flat, cols)
    par = partner.reshape(1, cols)

    def stay(x):
        return pltpu.with_memory_space_constraint(x, pltpu.HBM)

    vmem = pl.BlockSpec(memory_space=pltpu.VMEM)
    hbm = pl.BlockSpec(memory_space=pltpu.HBM)

    def shape(*dims):
        return jax.ShapeDtypeStruct(dims, F32)

    small = pltpu.CompilerParams(vmem_limit_bytes=(8 + n // 2) * 2**20)
    out, peer, depth, cp, th = pl.pallas_call(
        pack_kernel,
        out_shape=(
            shape(ROWS1, cols),
            shape(PEER1, cols),
            shape(rows, cols),
            shape(TALL, cols),
            shape(TALL, cols),
        ),
        in_specs=[hbm] * 8,
        out_specs=(vmem,) * 5,
        scratch_shapes=[
            pltpu.SMEM((count,), F32),
            pltpu.SMEM((count,), F32),
            pltpu.VMEM((flat, cols), F32),
            pltpu.VMEM((rows, cols), F32),
            pltpu.VMEM((steps, flat, cols), F32),
            pltpu.VMEM((steps, flat, cols), F32),
            pltpu.VMEM((rows, cols), jnp.int32),
            pltpu.VMEM((1, cols), jnp.int32),
            pltpu.SemaphoreType.DMA((8,)),
        ],
        compiler_params=small,
    )(*(stay(x) for x in (coupling, thickness, adj, adjoint_surface, u, v, levels, par)))
    both1, beyond1 = exchange(out, peer)
    temp, out, peer, kept = pl.pallas_call(
        first_kernel,
        out_shape=(
            shape(flat, cols),
            shape(ROWS2, cols),
            shape(PEER2, cols),
            shape(TALL + 8, cols),
        ),
        in_specs=[vmem] * 8,
        out_specs=(vmem,) * 4,
        scratch_shapes=[
            pltpu.VMEM((n, 2 * rows, cols), F32),
            pltpu.VMEM((n, cols), F32),
            pltpu.VMEM((2, TALL, cols), F32),
        ],
        compiler_params=small,
    )(cp, th, both1, beyond1, adj, u, v, depth)
    both, beyond = exchange(out, peer)
    temp_gradient, surface_gradient = pl.pallas_call(
        second_kernel,
        out_shape=(shape(flat, cols), shape(rows, cols)),
        in_specs=[vmem] * 10,
        out_specs=(vmem, vmem),
        scratch_shapes=[
            pltpu.VMEM((n, 2 * rows, cols), F32),
            pltpu.VMEM((n, cols), F32),
            pltpu.VMEM((3, TALL, cols), F32),
        ],
        compiler_params=small,
    )(th, both, beyond, both1, beyond1, kept, temp, u, v, depth)
    return temp_gradient.reshape(count, rows, cols), surface_gradient


def solution(mesh):
    return jax.shard_map(
        on_device,
        mesh=mesh,
        in_specs=(
            P("grp", "ja", "ia"),
            P(("grp", "ja"), "ia"),
            P(None, None, "ja", "ia"),
            P(None, None, "ja", "ia"),
            P("ja", "ia"),
            P("ia"),
            P(),
            P(),
        ),
        out_specs=(P("grp", "ja", "ia"), P(("grp", "ja"), "ia")),
        check_vma=False,
    )
```

```python
import jax
import jax.numpy as jnp
from jax import lax
from jax.experimental import pallas as pl
from jax.experimental.pallas import tpu as pltpu
from jax.sharding import PartitionSpec as P

SOLVER_ITERS = 2
SURFACE_COEF = 2.0
F32 = jnp.float32

EDGE1, ROWS1 = 16, 32
DEPTHS = 32
EDGE2, HROW2, LINE2, FLUX2, ROWS2 = 16, 24, 25, 50, 64
PEER1, PEER2 = 104, 32
WINDOW = 16
TALL = 32


def iota(shape, dim):
    return lax.broadcasted_iota(jnp.int32, shape, dim)


def full_sum(x):
    lines = jnp.sum(x.reshape(-1, 8, x.shape[-1]), axis=0)
    return jnp.sum(jnp.sum(lines, axis=0, keepdims=True), axis=1, keepdims=True)


def split_index(column, cols):
    return column >> (cols.bit_length() - 1), column & (cols - 1)


def fold_take(values, block, lane):
    out = jnp.zeros(block.shape, F32)
    for b in range(values.shape[0]):
        source = jnp.broadcast_to(values[b : b + 1], block.shape)
        out = jnp.where(block == b, jnp.take_along_axis(source, lane, axis=1), out)
    return out


def shift_blocks(x, step):
    return jnp.concatenate([x[step:], x[:step]], axis=0)


def surface_apply(field, block, lane):
    n, rows, cols = field.shape
    col = iota(field.shape, 2)
    row = iota(field.shape, 1)
    left = pltpu.roll(field, 1, 2)
    right = pltpu.roll(field, cols - 1, 2)
    west = jnp.where(col == 0, shift_blocks(left, n - 1), left)
    east = jnp.where(col == cols - 1, shift_blocks(right, 1), right)
    across = fold_take(field[:, rows - 1, :], block, lane)
    north = jnp.where(row == rows - 1, across[:, None, :], pltpu.roll(field, rows - 1, 1))
    south = jnp.where(row == 0, 0.0, pltpu.roll(field, 1, 1))
    return (1.0 + 4.0 * SURFACE_COEF) * field - SURFACE_COEF * (east + west + north + south)


def surface_solve(forcing, block, lane):
    applied = surface_apply(forcing, block, lane)
    again = surface_apply(applied, block, lane)
    norm = full_sum(forcing * forcing)
    step_size = norm / full_sum(forcing * applied)
    residual = forcing - step_size * applied
    ratio = full_sum(residual * residual) / norm
    direction = residual + ratio * forcing
    turned = (1.0 + ratio) * applied - step_size * again
    next_size = ratio * norm / full_sum(direction * turned)
    return step_size * forcing + next_size * direction


def level_rows(ref, base, count, rows):
    return ref[pl.ds(base, count, stride=rows), :]


def code_place(rows, cols):
    return rows - 2


def start_all(pairs, sems):
    copies = [pltpu.make_async_copy(src, dst, sems.at[i]) for i, (src, dst) in enumerate(pairs)]
    for copy in copies:
        copy.start()
    return copies


def pack_kernel(
    cp_in, th_in, adj_in, surf_in, u_in, v_in, lev_in, par_in, out, peer, depth_out, cp_out, th_out,
    cp, th, adj, surf, u, v, lev, par, sems
):
    copies = start_all(
        ((cp_in, cp), (lev_in, lev), (surf_in, surf), (par_in, par), (adj_in, adj), (u_in, u), (v_in, v), (th_in, th)),
        sems,
    )
    for copy in copies[:5]:
        copy.wait()
    rows, cols = surf.shape
    count = adj.shape[0] // rows
    top = lax.axis_index("ja") == lax.axis_size("ja") - 1
    lane = iota((rows, cols), 1)
    depth = lev[...].astype(F32)
    depth_out[...] = depth
    forcing = surf[...]
    last = cols - 1
    edge = jnp.where(lane == 4 * count, depth[:, last:], 0.0)
    edge = jnp.where(lane == 4 * count + 1, depth[:, :1], edge)
    for k in range(count):
        here = adj[k * rows : (k + 1) * rows, :]
        forcing = forcing + cp[k] * jnp.where(depth > k, here, 0.0)
        edge = jnp.where(lane == k, here[:, last:], edge)
        edge = jnp.where(lane == 3 * count + k, here[:, :1], edge)
    copies[5].wait()
    for k in range(count):
        u0 = u[0, k * rows : (k + 1) * rows, :]
        u1 = u[1, k * rows : (k + 1) * rows, :]
        edge = jnp.where(lane == count + k, u1[:, last:], edge)
        edge = jnp.where(lane == 2 * count + k, u0[:, last:], edge)
    width = cols // rows
    code = par[...].astype(F32) * DEPTHS + depth[rows - 1 :]
    taken = (iota((rows, cols), 0) * width + (lane & (width - 1))) & (cols - 1)
    spread = jnp.take_along_axis(jnp.broadcast_to(code, (rows, cols)), taken, axis=1)
    edge = jnp.where(lane // width == code_place(rows, cols), spread, edge)
    out[EDGE1 : EDGE1 + rows, :] = edge
    for copy in copies[6:]:
        copy.wait()
    cp_out[...] = level_column(cp, count, cols)
    th_out[...] = level_column(th, count, cols)
    out[0:rows, :] = forcing
    peer[...] = jnp.zeros(peer.shape, F32)
    is_top = jnp.full((count, cols), top.astype(jnp.int32)) == 1
    last_row = level_rows(adj, rows - 1, count, rows)
    peer[0:count, :] = jnp.where(is_top, level_rows(adj, 0, count, rows), last_row)
    peer[count : 2 * count, :] = v[1, pl.ds(rows - 1, count, stride=rows), :]
    peer[2 * count : 3 * count, :] = v[0, pl.ds(rows - 1, count, stride=rows), :]
    peer[3 * count : 4 * count, :] = last_row
    peer[4 * count : 4 * count + 1, :] = jnp.where(is_top[:1], depth[:1], depth[rows - 1 :])


def parity(x):
    for shift in (8, 4, 2, 1):
        x = x ^ (x >> shift)
    return x & 1


def exchange_steps(n, kind):
    steps = []
    while n > 1:
        n //= 2
        steps.append(n)
    return steps if kind == 0 else steps[:1] + steps[:0:-1]


def slot_of(distance, n, kind):
    out = 0
    for r, step in enumerate(exchange_steps(n, kind)):
        out = out | (((distance >> (step.bit_length() - 1)) & 1) << r)
    return out


class Messages:
    def __init__(self, both):
        self.both = both
        self.count = both.shape[1]
        self.me = lax.axis_index("ia")
        self.kind = parity(self.me) ^ lax.axis_index("ja")
        self.own = [slot_of(self.me, self.count, kind) for kind in range(2)]

    def part(self, block, core, start, stop):
        kind = parity(block) ^ core
        slot = self.own[kind] ^ slot_of(block, self.count, kind)
        return self.both[self.kind ^ kind, slot, start:stop, :]

    def beside(self, block, start, stop):
        kind = parity(block) ^ lax.axis_index("ja")
        away = block ^ self.me
        slot = jnp.where(
            kind == 0, slot_of(away, self.count, 0), slot_of(away, self.count, 1)
        )
        return self.both[self.kind ^ kind, slot, start:stop, :]

    def field(self, rows):
        blocks = [
            jnp.concatenate([self.part(b, 0, 0, rows), self.part(b, 1, 0, rows)], axis=0)
            for b in range(self.count)
        ]
        return jnp.stack(blocks, axis=0)

    def codes(self, rows, out):
        cols = self.both.shape[3]
        width = cols // rows
        lane = iota((rows, cols), 1)
        taken = code_place(rows, cols) * width + (lane & (width - 1))
        here = lane // width == iota((rows, cols), 0)
        for b in range(self.count):
            edge = self.part(b, 1, EDGE1, EDGE1 + rows)
            moved = jnp.where(here, jnp.take_along_axis(edge, taken, axis=1), 0.0)
            out[b : b + 1, :] = jnp.sum(moved, axis=0, keepdims=True)
        return out[...].astype(jnp.int32)

    def line(self, core, index, out):
        for b in range(self.count):
            out[b : b + 1, :] = self.part(b, core, index, index + 1)
        return out[...]


def level_column(values, count, cols):
    level = iota((TALL, cols), 0)
    out = jnp.zeros((TALL, cols), F32)
    for k in range(count):
        out = jnp.where(level == k, values[k], out)
    return out


def position(n):
    me = lax.axis_index("ia")
    return me, lax.rem(me + n - 1, n), lax.rem(me + 1, n)


def sweep_levels(count, rows, th, fetch, west_of, east_of, u, v, pieces, top, depth, masks, emit):
    own, left, right, beside, beside_temp, beside_v = pieces
    east_depth, west_depth, north_depth, south_depth = masks
    cols = own.shape[1]
    lane = iota((rows, cols), 1)
    row = iota((rows, cols), 0)
    is_top = jnp.full((1, cols), top.astype(jnp.int32)) == 1
    for k in range(count):
        here = fetch(k)
        weight = th[k : k + 1, :]
        add = weight * own
        mid = here + jnp.where(depth > k, add, 0.0)
        bare = here + add
        u_west, t_west = west_of(k)
        west_value = t_west + weight * left
        east_value = jnp.where(
            lane == cols - 1, east_of(k) + weight * right, pltpu.roll(bare, cols - 1, 1)
        )
        u_here = u[k * rows : (k + 1) * rows, :]
        v_here = v[k * rows : (k + 1) * rows, :]
        flux_east = jnp.where(east_depth > k, 0.25 * u_here * (east_value - bare), 0.0)
        flux_first = jnp.where(west_depth > k, 0.25 * u_west * (bare - west_value), 0.0)
        flux_west = jnp.where(lane == 0, flux_first, pltpu.roll(flux_east, 1, 1))
        beside_value = beside_temp(k) + weight * beside
        above = jnp.where(is_top, 0.0, beside_value)
        north_value = jnp.where(row == rows - 1, above, pltpu.roll(bare, rows - 1, 0))
        flux_north = jnp.where(north_depth > k, 0.25 * v_here * (north_value - bare), 0.0)
        flux_below = jnp.where(south_depth > k, 0.25 * beside_v(k) * (bare[:1] - beside_value), 0.0)
        flux_south = jnp.where(row == 0, flux_below, pltpu.roll(flux_north, 1, 0))
        emit(k, mid + flux_east + flux_west + flux_north + flux_south)


def face_depths(depth, edge_left, edge_right, beside_depth, count, top):
    rows, cols = depth.shape
    lane = iota(depth.shape, 1)
    row = iota(depth.shape, 0)
    is_top = jnp.full(depth.shape, top.astype(jnp.int32)) == 1
    right = edge_right[:, 4 * count + 1 : 4 * count + 2]
    east = jnp.minimum(depth, jnp.where(lane == cols - 1, right, pltpu.roll(depth, cols - 1, 1)))
    west = jnp.minimum(depth, edge_left[:, 4 * count : 4 * count + 1])
    above = jnp.where(is_top, depth, beside_depth)
    north = jnp.minimum(depth, jnp.where(row == rows - 1, above, pltpu.roll(depth, rows - 1, 0)))
    south = jnp.where(is_top[:1], jnp.minimum(depth[:1], beside_depth), 0.0)
    return east, west, north, south


def load_pieces(solved, me, west, east, rows, top):
    cols = solved.shape[-1]
    here = pl.ds(pl.multiple_of(jnp.where(top, rows, 0), 8), rows)
    own = solved[me, here, :]
    left = pltpu.roll(solved[west, here, :], 1, 1)
    right = pltpu.roll(solved[east, here, :], cols - 1, 1)
    is_top = jnp.full((1, cols), top.astype(jnp.int32)) == 1
    block = solved[me]
    beside = jnp.where(is_top, block[rows - 1 : rows], block[rows : rows + 1])
    return own, left, right, beside


def first_kernel(
    cp, th, both, beyond, adj, u_in, v_in, depth_in, t_out, out, peer, kept, table, solved, rowbuf, tall
):
    u, v = u_in.at[1], v_in.at[1]
    rows, cols = depth_in.shape
    count = adj.shape[0] // rows
    top = lax.axis_index("ja") == lax.axis_size("ja") - 1
    sent = Messages(both)
    me, west, east = position(sent.count)
    code = sent.codes(rows, rowbuf)
    partner = code >> (DEPTHS.bit_length() - 1)
    table[...] = partner
    block, lane = split_index(partner, cols)
    solved[...] = surface_solve(sent.field(rows), block, lane)
    depths = (code & (DEPTHS - 1)).astype(F32)
    rowbuf[...] = depths
    fold_depth = rowbuf[pl.ds(me, 1), :]
    rowbuf[...] = fold_take(depths, block, lane)
    across_depth = rowbuf[pl.ds(me, 1), :]

    is_top = jnp.full((count, cols), top.astype(jnp.int32)) == 1
    level = iota((TALL, cols), 0).astype(F32)
    tall[0, 0:count, :] = jnp.where(
        is_top, level_rows(v, rows - 1, count, rows), beyond[count : 2 * count, :]
    )
    tall[1, 0:count, :] = jnp.where(
        is_top, level_rows(adj, rows - 1, count, rows), beyond[3 * count : 4 * count, :]
    )
    fold_solved = solved[me, 2 * rows - 8 :, :][7:]
    flux = jnp.where(
        fold_depth > level,
        0.25 * tall[0] * (tall[1] + th[...] * fold_solved),
        0.0,
    )
    into = jnp.where(across_depth > level, cp[...] * flux, 0.0)
    kept[0:TALL, :] = flux
    kept[TALL:, :] = jnp.broadcast_to(across_depth, (8, cols))
    out[HROW2 : HROW2 + 1, :] = jnp.sum(into, axis=0, keepdims=True)

    depth = depth_in[...]
    edge_left = sent.beside(west, EDGE1, EDGE1 + rows)
    edge_right = sent.beside(east, EDGE1, EDGE1 + rows)
    beside_depth = beyond[4 * count : 4 * count + 1, :]
    masks = face_depths(depth, edge_left, edge_right, beside_depth, count, top)
    own, left, right, beside = load_pieces(solved, me, west, east, rows, top)
    pieces = (
        own,
        left,
        right,
        beside,
        lambda k: beyond[k : k + 1, :],
        lambda k: beyond[count + k : count + k + 1, :],
    )
    spot = iota((rows, cols), 1)
    carry = {"forcing": own, "edge": jnp.zeros((rows, cols), F32)}

    def emit(k, value):
        t_out[k * rows : (k + 1) * rows, :] = value
        carry["forcing"] = carry["forcing"] + cp[k : k + 1, :] * jnp.where(depth > k, value, 0.0)
        edge = jnp.where(spot == k, value[:, cols - 1 :], carry["edge"])
        carry["edge"] = jnp.where(spot == count + k, value[:, :1], edge)

    sweep_levels(
        count,
        rows,
        th,
        lambda k: adj[k * rows : (k + 1) * rows, :],
        lambda k: (edge_left[:, count + k : count + k + 1], edge_left[:, k : k + 1]),
        lambda k: edge_right[:, 3 * count + k : 3 * count + k + 1],
        u,
        v,
        pieces,
        top,
        depth,
        masks,
        emit,
    )
    out[0:rows, :] = carry["forcing"]
    half = rows // 2
    edge = carry["edge"]
    out[EDGE2 : EDGE2 + half, :] = jnp.where(
        spot[:half] < cols // 2, edge[:half], pltpu.roll(edge[half:], cols // 2, 1)
    )
    last_row = level_rows(t_out, rows - 1, count, rows)
    out[LINE2 : LINE2 + count, :] = jnp.where(is_top, last_row, beyond[2 * count : 3 * count, :])
    later, share = count // 2, count - count // 2
    out[FLUX2 : FLUX2 + share, :] = jnp.where(
        is_top[:share], kept[later:count, :], kept[0:share, :]
    )
    out[FLUX2 + share :, :] = jnp.zeros((ROWS2 - FLUX2 - share, cols), F32)
    peer[0:count, :] = jnp.where(is_top, level_rows(t_out, 0, count, rows), last_row)
    peer[count:, :] = jnp.zeros((peer.shape[0] - count, cols), F32)


def second_kernel(
    th, both, beyond, both1, beyond1, kept, table, temp, u_in, v_in, depth_in, t_out, s_out, solved, rowbuf, tall
):
    u, v = u_in.at[0], v_in.at[0]
    rows, cols = depth_in.shape
    count = temp.shape[0] // rows
    top = lax.axis_index("ja") == lax.axis_size("ja") - 1
    sent, sent1 = Messages(both), Messages(both1)
    n = sent.count
    me, west, east = position(n)
    partner = table[...]
    block, lane = split_index(partner, cols)
    forcing = sent.field(rows)
    fold = fold_take(sent.line(0, HROW2, rowbuf), block, lane)
    row3 = iota(forcing.shape, 1)
    forcing = forcing - jnp.where(row3 == 2 * rows - 1, fold[:, None, :], 0.0)
    iterate = surface_solve(forcing, block, lane)
    solved[...] = iterate
    rowbuf[...] = fold_take(iterate[:, 2 * rows - 1, :], block, lane)
    across_solved = rowbuf[pl.ds(me, 1), :]

    spot = iota((1, cols), 1)
    rowbuf[...] = partner.astype(F32)
    beside_left = pltpu.roll(rowbuf[pl.ds(west, 1), :], 1, 1)
    beside_right = pltpu.roll(rowbuf[pl.ds(east, 1), :], cols - 1, 1)
    end_partner = jnp.where(spot == 0, beside_left, beside_right)
    end_partner = jnp.where((spot == 0) | (spot == cols - 1), end_partner, 0.0)
    own_partner = jnp.broadcast_to(rowbuf[pl.ds(me, 1), :], (TALL, cols)).astype(jnp.int32)
    end_partner = jnp.broadcast_to(end_partner, (WINDOW, cols)).astype(jnp.int32)
    own_block, own_lane = split_index(own_partner, cols)
    end_block, end_lane = split_index(end_partner, cols)
    zero, low = jnp.zeros((TALL, cols), F32), jnp.zeros((WINDOW, cols), F32)
    temp_across, v_across = zero, zero
    own_flux, end_flux = [low, low], [low, low]
    for b in range(n):
        here, there = own_block == b, end_block == b
        line = sent.part(b, 1, LINE2, LINE2 + TALL)
        temp_across = jnp.where(here, jnp.take_along_axis(line, own_lane, axis=1), temp_across)
        line = sent.part(b, 0, LINE2, LINE2 + TALL)
        v_across = jnp.where(here, jnp.take_along_axis(line, own_lane, axis=1), v_across)
        for c in range(2):
            line = sent.part(b, c, ROWS2 - WINDOW, ROWS2)
            moved = jnp.take_along_axis(line, own_lane[:WINDOW], axis=1)
            own_flux[c] = jnp.where(here[:WINDOW], moved, own_flux[c])
            moved = jnp.take_along_axis(line, end_lane, axis=1)
            end_flux[c] = jnp.where(there, moved, end_flux[c])
    skip = FLUX2 - (ROWS2 - WINDOW)
    later, share = count // 2, count - count // 2
    for i, parts in enumerate((own_flux, end_flux)):
        for c, start in ((0, 0), (1, later)):
            tall[2, 0:WINDOW, :] = parts[c]
            tall[i, start : start + share, :] = tall[2, skip : skip + share, :]
    level = iota((TALL, cols), 0).astype(F32)
    fold_last = jnp.where(
        kept[TALL : TALL + 1, :] > level,
        0.25
        * v_across
        * (temp_across - kept[0:TALL, :] + th[...] * across_solved),
        0.0,
    )
    tall[2] = fold_last

    depth = depth_in[...]
    edge1_left = sent1.beside(west, EDGE1, EDGE1 + rows)
    edge1_right = sent1.beside(east, EDGE1, EDGE1 + rows)
    half = rows // 2

    def both_rows(line):
        return jnp.concatenate([line, pltpu.roll(line, cols // 2, 1)], axis=0)

    edge_left = both_rows(sent.beside(west, EDGE2, EDGE2 + half))
    edge_right = both_rows(sent.beside(east, EDGE2, EDGE2 + half))
    beside_depth = beyond1[4 * count : 4 * count + 1, :]
    masks = face_depths(depth, edge1_left, edge1_right, beside_depth, count, top)
    own, left, right, beside = load_pieces(solved, me, west, east, rows, top)
    s_out[...] = own
    pieces = (
        own,
        left,
        right,
        beside,
        lambda k: beyond[k : k + 1, :],
        lambda k: beyond1[2 * count + k : 2 * count + k + 1, :],
    )
    row = iota((rows, cols), 0)
    on_fold = (row == rows - 1) & (jnp.full((rows, cols), top.astype(jnp.int32)) == 1)

    def less(value, index, k):
        return value - jnp.where(on_fold, tall[index, k : k + 1, :], 0.0)

    def emit(k, value):
        t_out[k * rows : (k + 1) * rows, :] = less(value, 2, k)

    def spread(column):
        return jnp.broadcast_to(column, (rows, cols))

    sweep_levels(
        count,
        rows,
        th,
        lambda k: less(temp[k * rows : (k + 1) * rows, :], 0, k),
        lambda k: (
            edge1_left[:, 2 * count + k : 2 * count + k + 1],
            less(spread(edge_left[:, k : k + 1]), 1, k),
        ),
        lambda k: less(spread(edge_right[:, count + k : count + k + 1]), 1, k),
        u,
        v,
        pieces,
        top,
        depth,
        masks,
        emit,
    )


def exchange(block, peer):
    n = lax.axis_size("ia")
    rows, cols = block.shape
    kinds = [exchange_steps(n, kind) for kind in range(2)]
    y = block
    for near, far in zip(*kinds):
        pairs = []
        for i in range(n):
            for c in range(2):
                step = far if parity(i) ^ c else near
                pairs.append((2 * i + c, 2 * (i ^ step) + 1 - c))
        y = jnp.concatenate([y, lax.ppermute(y, ("ia", "ja"), pairs)])
    z = lax.ppermute(jnp.concatenate([y, peer]), "ja", [(0, 1), (1, 0)])
    both = jnp.concatenate([y, z[: n * rows]]).reshape(2, n, rows, cols)
    return both, z[n * rows :]


def on_device(
    adjoint_temp, adjoint_surface, trajectory_u, trajectory_v, levels, partner, thickness, coupling
):
    steps, count, rows, cols = trajectory_u.shape
    n = lax.axis_size("ia")
    flat = count * rows
    adj = adjoint_temp.reshape(flat, cols)
    u = trajectory_u.reshape(steps, flat, cols)
    v = trajectory_v.reshape(steps, flat, cols)
    par = partner.reshape(1, cols)

    def stay(x):
        return pltpu.with_memory_space_constraint(x, pltpu.HBM)

    vmem = pl.BlockSpec(memory_space=pltpu.VMEM)
    hbm = pl.BlockSpec(memory_space=pltpu.HBM)

    def shape(*dims):
        return jax.ShapeDtypeStruct(dims, F32)

    small = pltpu.CompilerParams(vmem_limit_bytes=(8 + n // 2) * 2**20)
    out, peer, depth, cp, th = pl.pallas_call(
        pack_kernel,
        out_shape=(
            shape(ROWS1, cols),
            shape(PEER1, cols),
            shape(rows, cols),
            shape(TALL, cols),
            shape(TALL, cols),
        ),
        in_specs=[hbm] * 8,
        out_specs=(vmem,) * 5,
        scratch_shapes=[
            pltpu.SMEM((count,), F32),
            pltpu.SMEM((count,), F32),
            pltpu.VMEM((flat, cols), F32),
            pltpu.VMEM((rows, cols), F32),
            pltpu.VMEM((steps, flat, cols), F32),
            pltpu.VMEM((steps, flat, cols), F32),
            pltpu.VMEM((rows, cols), jnp.int32),
            pltpu.VMEM((1, cols), jnp.int32),
            pltpu.SemaphoreType.DMA((8,)),
        ],
        compiler_params=small,
    )(*(stay(x) for x in (coupling, thickness, adj, adjoint_surface, u, v, levels, par)))
    both1, beyond1 = exchange(out, peer)
    temp, out, peer, kept, table = pl.pallas_call(
        first_kernel,
        out_shape=(
            shape(flat, cols),
            shape(ROWS2, cols),
            shape(PEER2, cols),
            shape(TALL + 8, cols),
            jax.ShapeDtypeStruct((n, cols), jnp.int32),
        ),
        in_specs=[vmem] * 8,
        out_specs=(vmem,) * 5,
        scratch_shapes=[
            pltpu.VMEM((n, 2 * rows, cols), F32),
            pltpu.VMEM((n, cols), F32),
            pltpu.VMEM((2, TALL, cols), F32),
        ],
        compiler_params=small,
    )(cp, th, both1, beyond1, adj, u, v, depth)
    both, beyond = exchange(out, peer)
    temp_gradient, surface_gradient = pl.pallas_call(
        second_kernel,
        out_shape=(shape(flat, cols), shape(rows, cols)),
        in_specs=[vmem] * 11,
        out_specs=(vmem, vmem),
        scratch_shapes=[
            pltpu.VMEM((n, 2 * rows, cols), F32),
            pltpu.VMEM((n, cols), F32),
            pltpu.VMEM((3, TALL, cols), F32),
        ],
        compiler_params=small,
    )(th, both, beyond, both1, beyond1, kept, table, temp, u, v, depth)
    return temp_gradient.reshape(count, rows, cols), surface_gradient


def solution(mesh):
    return jax.shard_map(
        on_device,
        mesh=mesh,
        in_specs=(
            P("grp", "ja", "ia"),
            P(("grp", "ja"), "ia"),
            P(None, None, "ja", "ia"),
            P(None, None, "ja", "ia"),
            P("ja", "ia"),
            P("ia"),
            P(),
            P(),
        ),
        out_specs=(P("grp", "ja", "ia"), P(("grp", "ja"), "ia")),
        check_vma=False,
    )
```

```python
import jax
import jax.numpy as jnp
from jax import lax
from jax.experimental import pallas as pl
from jax.experimental.pallas import tpu as pltpu
from jax.sharding import PartitionSpec as P

SOLVER_ITERS = 2
SURFACE_COEF = 2.0
F32 = jnp.float32

EDGE1, ROWS1 = 16, 32
DEPTHS = 32
EDGE2, HROW2, LINE2, FLUX2, ROWS2 = 16, 24, 25, 50, 64
PEER1, PEER2 = 104, 32
WINDOW = 16
TALL = 32


def iota(shape, dim):
    return lax.broadcasted_iota(jnp.int32, shape, dim)


def full_sum(x):
    lines = jnp.sum(x.reshape(-1, 8, x.shape[-1]), axis=0)
    return jnp.sum(jnp.sum(lines, axis=1, keepdims=True), axis=0, keepdims=True)


def split_index(column, cols):
    return column >> (cols.bit_length() - 1), column & (cols - 1)


def fold_take(values, block, lane):
    out = jnp.zeros(block.shape, F32)
    for b in range(values.shape[0]):
        source = jnp.broadcast_to(values[b : b + 1], block.shape)
        out = jnp.where(block == b, jnp.take_along_axis(source, lane, axis=1), out)
    return out


def shift_blocks(x, step):
    return jnp.concatenate([x[step:], x[:step]], axis=0)


def surface_apply(field, block, lane):
    n, rows, cols = field.shape
    col = iota(field.shape, 2)
    row = iota(field.shape, 1)
    left = pltpu.roll(field, 1, 2)
    right = pltpu.roll(field, cols - 1, 2)
    west = jnp.where(col == 0, shift_blocks(left, n - 1), left)
    east = jnp.where(col == cols - 1, shift_blocks(right, 1), right)
    across = fold_take(field[:, rows - 1, :], block, lane)
    north = jnp.where(row == rows - 1, across[:, None, :], pltpu.roll(field, rows - 1, 1))
    south = jnp.where(row == 0, 0.0, pltpu.roll(field, 1, 1))
    return (1.0 + 4.0 * SURFACE_COEF) * field - SURFACE_COEF * (east + west + north + south)


def surface_solve(forcing, block, lane):
    applied = surface_apply(forcing, block, lane)
    again = surface_apply(applied, block, lane)
    norm = full_sum(forcing * forcing)
    step_size = norm / full_sum(forcing * applied)
    residual = forcing - step_size * applied
    ratio = full_sum(residual * residual) / norm
    direction = residual + ratio * forcing
    turned = (1.0 + ratio) * applied - step_size * again
    next_size = ratio * norm / full_sum(direction * turned)
    return step_size * forcing + next_size * direction


def level_rows(ref, base, count, rows):
    return ref[pl.ds(base, count, stride=rows), :]


def code_place(rows, cols):
    return rows - 2


def start_all(pairs, sems):
    copies = [pltpu.make_async_copy(src, dst, sems.at[i]) for i, (src, dst) in enumerate(pairs)]
    for copy in copies:
        copy.start()
    return copies


def pack_kernel(
    cp_in, th_in, adj_in, surf_in, u_in, v_in, lev_in, par_in, out, peer, depth_out, cp_out, th_out,
    cp, th, adj, surf, u, v, lev, par, sems
):
    copies = start_all(
        ((cp_in, cp), (lev_in, lev), (surf_in, surf), (par_in, par), (adj_in, adj), (u_in, u), (v_in, v), (th_in, th)),
        sems,
    )
    for copy in copies[:5]:
        copy.wait()
    rows, cols = surf.shape
    count = adj.shape[0] // rows
    top = lax.axis_index("ja") == lax.axis_size("ja") - 1
    lane = iota((rows, cols), 1)
    depth = lev[...].astype(F32)
    depth_out[...] = depth
    forcing = surf[...]
    last = cols - 1
    edge = jnp.where(lane == 4 * count, depth[:, last:], 0.0)
    edge = jnp.where(lane == 4 * count + 1, depth[:, :1], edge)
    for k in range(count):
        here = adj[k * rows : (k + 1) * rows, :]
        forcing = forcing + cp[k] * jnp.where(depth > k, here, 0.0)
        edge = jnp.where(lane == k, here[:, last:], edge)
        edge = jnp.where(lane == 3 * count + k, here[:, :1], edge)
    copies[5].wait()
    for k in range(count):
        u0 = u[0, k * rows : (k + 1) * rows, :]
        u1 = u[1, k * rows : (k + 1) * rows, :]
        edge = jnp.where(lane == count + k, u1[:, last:], edge)
        edge = jnp.where(lane == 2 * count + k, u0[:, last:], edge)
    width = cols // rows
    code = par[...].astype(F32) * DEPTHS + depth[rows - 1 :]
    taken = (iota((rows, cols), 0) * width + (lane & (width - 1))) & (cols - 1)
    spread = jnp.take_along_axis(jnp.broadcast_to(code, (rows, cols)), taken, axis=1)
    edge = jnp.where(lane // width == code_place(rows, cols), spread, edge)
    out[EDGE1 : EDGE1 + rows, :] = edge
    for copy in copies[6:]:
        copy.wait()
    cp_out[...] = level_column(cp, count, cols)
    th_out[...] = level_column(th, count, cols)
    out[0:rows, :] = forcing
    peer[...] = jnp.zeros(peer.shape, F32)
    is_top = jnp.full((count, cols), top.astype(jnp.int32)) == 1
    last_row = level_rows(adj, rows - 1, count, rows)
    peer[0:count, :] = jnp.where(is_top, level_rows(adj, 0, count, rows), last_row)
    peer[count : 2 * count, :] = v[1, pl.ds(rows - 1, count, stride=rows), :]
    peer[2 * count : 3 * count, :] = v[0, pl.ds(rows - 1, count, stride=rows), :]
    peer[3 * count : 4 * count, :] = last_row
    peer[4 * count : 4 * count + 1, :] = jnp.where(is_top[:1], depth[:1], depth[rows - 1 :])


def parity(x):
    for shift in (8, 4, 2, 1):
        x = x ^ (x >> shift)
    return x & 1


def exchange_steps(n, kind):
    steps = []
    while n > 1:
        n //= 2
        steps.append(n)
    return steps if kind == 0 else steps[:1] + steps[:0:-1]


def slot_of(distance, n, kind):
    out = 0
    for r, step in enumerate(exchange_steps(n, kind)):
        out = out | (((distance >> (step.bit_length() - 1)) & 1) << r)
    return out


class Messages:
    def __init__(self, both):
        self.both = both
        self.count = both.shape[1]
        self.me = lax.axis_index("ia")
        self.kind = parity(self.me) ^ lax.axis_index("ja")
        self.own = [slot_of(self.me, self.count, kind) for kind in range(2)]

    def part(self, block, core, start, stop):
        kind = parity(block) ^ core
        slot = self.own[kind] ^ slot_of(block, self.count, kind)
        return self.both[self.kind ^ kind, slot, start:stop, :]

    def beside(self, block, start, stop):
        kind = parity(block) ^ lax.axis_index("ja")
        away = block ^ self.me
        slot = jnp.where(
            kind == 0, slot_of(away, self.count, 0), slot_of(away, self.count, 1)
        )
        return self.both[self.kind ^ kind, slot, start:stop, :]

    def field(self, rows):
        blocks = [
            jnp.concatenate([self.part(b, 0, 0, rows), self.part(b, 1, 0, rows)], axis=0)
            for b in range(self.count)
        ]
        return jnp.stack(blocks, axis=0)

    def codes(self, rows, out):
        cols = self.both.shape[3]
        width = cols // rows
        lane = iota((rows, cols), 1)
        taken = code_place(rows, cols) * width + (lane & (width - 1))
        here = lane // width == iota((rows, cols), 0)
        for b in range(self.count):
            edge = self.part(b, 1, EDGE1, EDGE1 + rows)
            moved = jnp.where(here, jnp.take_along_axis(edge, taken, axis=1), 0.0)
            out[b : b + 1, :] = jnp.sum(moved, axis=0, keepdims=True)
        return out[...].astype(jnp.int32)

    def line(self, core, index, out):
        for b in range(self.count):
            out[b : b + 1, :] = self.part(b, core, index, index + 1)
        return out[...]


def level_column(values, count, cols):
    level = iota((TALL, cols), 0)
    out = jnp.zeros((TALL, cols), F32)
    for k in range(count):
        out = jnp.where(level == k, values[k], out)
    return out


def position(n):
    me = lax.axis_index("ia")
    return me, lax.rem(me + n - 1, n), lax.rem(me + 1, n)


def sweep_levels(count, rows, th, fetch, west_of, east_of, u, v, pieces, top, depth, masks, emit):
    own, left, right, beside, beside_temp, beside_v = pieces
    east_depth, west_depth, north_depth, south_depth = masks
    cols = own.shape[1]
    lane = iota((rows, cols), 1)
    row = iota((rows, cols), 0)
    is_top = jnp.full((1, cols), top.astype(jnp.int32)) == 1
    for k in range(count):
        here = fetch(k)
        weight = th[k : k + 1, :]
        add = weight * own
        mid = here + jnp.where(depth > k, add, 0.0)
        bare = here + add
        u_west, t_west = west_of(k)
        west_value = t_west + weight * left
        east_value = jnp.where(
            lane == cols - 1, east_of(k) + weight * right, pltpu.roll(bare, cols - 1, 1)
        )
        u_here = u[k * rows : (k + 1) * rows, :]
        v_here = v[k * rows : (k + 1) * rows, :]
        flux_east = jnp.where(east_depth > k, 0.25 * u_here * (east_value - bare), 0.0)
        flux_first = jnp.where(west_depth > k, 0.25 * u_west * (bare - west_value), 0.0)
        flux_west = jnp.where(lane == 0, flux_first, pltpu.roll(flux_east, 1, 1))
        beside_value = beside_temp(k) + weight * beside
        above = jnp.where(is_top, 0.0, beside_value)
        north_value = jnp.where(row == rows - 1, above, pltpu.roll(bare, rows - 1, 0))
        flux_north = jnp.where(north_depth > k, 0.25 * v_here * (north_value - bare), 0.0)
        flux_below = jnp.where(south_depth > k, 0.25 * beside_v(k) * (bare[:1] - beside_value), 0.0)
        flux_south = jnp.where(row == 0, flux_below, pltpu.roll(flux_north, 1, 0))
        emit(k, mid + flux_east + flux_west + flux_north + flux_south)


def face_depths(depth, edge_left, edge_right, beside_depth, count, top):
    rows, cols = depth.shape
    lane = iota(depth.shape, 1)
    row = iota(depth.shape, 0)
    is_top = jnp.full(depth.shape, top.astype(jnp.int32)) == 1
    right = edge_right[:, 4 * count + 1 : 4 * count + 2]
    east = jnp.minimum(depth, jnp.where(lane == cols - 1, right, pltpu.roll(depth, cols - 1, 1)))
    west = jnp.minimum(depth, edge_left[:, 4 * count : 4 * count + 1])
    above = jnp.where(is_top, depth, beside_depth)
    north = jnp.minimum(depth, jnp.where(row == rows - 1, above, pltpu.roll(depth, rows - 1, 0)))
    south = jnp.where(is_top[:1], jnp.minimum(depth[:1], beside_depth), 0.0)
    return east, west, north, south


def load_pieces(solved, me, west, east, rows, top):
    cols = solved.shape[-1]
    here = pl.ds(pl.multiple_of(jnp.where(top, rows, 0), 8), rows)
    own = solved[me, here, :]
    left = pltpu.roll(solved[west, here, :], 1, 1)
    right = pltpu.roll(solved[east, here, :], cols - 1, 1)
    is_top = jnp.full((1, cols), top.astype(jnp.int32)) == 1
    block = solved[me]
    beside = jnp.where(is_top, block[rows - 1 : rows], block[rows : rows + 1])
    return own, left, right, beside


def first_kernel(
    cp, th, both, beyond, adj, u_in, v_in, depth_in, t_out, out, peer, kept, table, solved, rowbuf, tall
):
    u, v = u_in.at[1], v_in.at[1]
    rows, cols = depth_in.shape
    count = adj.shape[0] // rows
    top = lax.axis_index("ja") == lax.axis_size("ja") - 1
    sent = Messages(both)
    me, west, east = position(sent.count)
    code = sent.codes(rows, rowbuf)
    partner = code >> (DEPTHS.bit_length() - 1)
    table[...] = partner
    block, lane = split_index(partner, cols)
    solved[...] = surface_solve(sent.field(rows), block, lane)
    depths = (code & (DEPTHS - 1)).astype(F32)
    rowbuf[...] = depths
    fold_depth = rowbuf[pl.ds(me, 1), :]
    rowbuf[...] = fold_take(depths, block, lane)
    across_depth = rowbuf[pl.ds(me, 1), :]

    is_top = jnp.full((count, cols), top.astype(jnp.int32)) == 1
    level = iota((TALL, cols), 0).astype(F32)
    tall[0, 0:count, :] = jnp.where(
        is_top, level_rows(v, rows - 1, count, rows), beyond[count : 2 * count, :]
    )
    tall[1, 0:count, :] = jnp.where(
        is_top, level_rows(adj, rows - 1, count, rows), beyond[3 * count : 4 * count, :]
    )
    fold_solved = solved[me, 2 * rows - 8 :, :][7:]
    flux = jnp.where(
        fold_depth > level,
        0.25 * tall[0] * (tall[1] + th[...] * fold_solved),
        0.0,
    )
    into = jnp.where(across_depth > level, cp[...] * flux, 0.0)
    kept[0:TALL, :] = flux
    kept[TALL:, :] = jnp.broadcast_to(across_depth, (8, cols))
    out[HROW2 : HROW2 + 1, :] = jnp.sum(into, axis=0, keepdims=True)

    depth = depth_in[...]
    edge_left = sent.beside(west, EDGE1, EDGE1 + rows)
    edge_right = sent.beside(east, EDGE1, EDGE1 + rows)
    beside_depth = beyond[4 * count : 4 * count + 1, :]
    masks = face_depths(depth, edge_left, edge_right, beside_depth, count, top)
    own, left, right, beside = load_pieces(solved, me, west, east, rows, top)
    pieces = (
        own,
        left,
        right,
        beside,
        lambda k: beyond[k : k + 1, :],
        lambda k: beyond[count + k : count + k + 1, :],
    )
    spot = iota((rows, cols), 1)
    carry = {"forcing": own, "edge": jnp.zeros((rows, cols), F32)}

    def emit(k, value):
        t_out[k * rows : (k + 1) * rows, :] = value
        carry["forcing"] = carry["forcing"] + cp[k : k + 1, :] * jnp.where(depth > k, value, 0.0)
        edge = jnp.where(spot == k, value[:, cols - 1 :], carry["edge"])
        carry["edge"] = jnp.where(spot == count + k, value[:, :1], edge)

    sweep_levels(
        count,
        rows,
        th,
        lambda k: adj[k * rows : (k + 1) * rows, :],
        lambda k: (edge_left[:, count + k : count + k + 1], edge_left[:, k : k + 1]),
        lambda k: edge_right[:, 3 * count + k : 3 * count + k + 1],
        u,
        v,
        pieces,
        top,
        depth,
        masks,
        emit,
    )
    out[0:rows, :] = carry["forcing"]
    half = rows // 2
    edge = carry["edge"]
    out[EDGE2 : EDGE2 + half, :] = jnp.where(
        spot[:half] < cols // 2, edge[:half], pltpu.roll(edge[half:], cols // 2, 1)
    )
    last_row = level_rows(t_out, rows - 1, count, rows)
    out[LINE2 : LINE2 + count, :] = jnp.where(is_top, last_row, beyond[2 * count : 3 * count, :])
    later, share = count // 2, count - count // 2
    out[FLUX2 : FLUX2 + share, :] = jnp.where(
        is_top[:share], kept[later:count, :], kept[0:share, :]
    )
    out[FLUX2 + share :, :] = jnp.zeros((ROWS2 - FLUX2 - share, cols), F32)
    peer[0:count, :] = jnp.where(is_top, level_rows(t_out, 0, count, rows), last_row)
    peer[count:, :] = jnp.zeros((peer.shape[0] - count, cols), F32)


def second_kernel(
    th, both, beyond, both1, beyond1, kept, table, temp, u_in, v_in, depth_in, t_out, s_out, solved, rowbuf, tall
):
    u, v = u_in.at[0], v_in.at[0]
    rows, cols = depth_in.shape
    count = temp.shape[0] // rows
    top = lax.axis_index("ja") == lax.axis_size("ja") - 1
    sent, sent1 = Messages(both), Messages(both1)
    n = sent.count
    me, west, east = position(n)
    partner = table[...]
    block, lane = split_index(partner, cols)
    forcing = sent.field(rows)
    fold = fold_take(sent.line(0, HROW2, rowbuf), block, lane)
    row3 = iota(forcing.shape, 1)
    forcing = forcing - jnp.where(row3 == 2 * rows - 1, fold[:, None, :], 0.0)
    spot = iota((1, cols), 1)
    rowbuf[...] = partner.astype(F32)
    beside_left = pltpu.roll(rowbuf[pl.ds(west, 1), :], 1, 1)
    beside_right = pltpu.roll(rowbuf[pl.ds(east, 1), :], cols - 1, 1)
    end_partner = jnp.where(spot == 0, beside_left, beside_right)
    end_partner = jnp.where((spot == 0) | (spot == cols - 1), end_partner, 0.0)
    own_partner = jnp.broadcast_to(rowbuf[pl.ds(me, 1), :], (TALL, cols)).astype(jnp.int32)
    end_partner = jnp.broadcast_to(end_partner, (WINDOW, cols)).astype(jnp.int32)
    own_block, own_lane = split_index(own_partner, cols)
    end_block, end_lane = split_index(end_partner, cols)
    zero, low = jnp.zeros((TALL, cols), F32), jnp.zeros((WINDOW, cols), F32)
    temp_across, v_across = zero, zero
    own_flux, end_flux = [low, low], [low, low]
    for b in range(n):
        here, there = own_block == b, end_block == b
        line = sent.part(b, 1, LINE2, LINE2 + TALL)
        temp_across = jnp.where(here, jnp.take_along_axis(line, own_lane, axis=1), temp_across)
        line = sent.part(b, 0, LINE2, LINE2 + TALL)
        v_across = jnp.where(here, jnp.take_along_axis(line, own_lane, axis=1), v_across)
        for c in range(2):
            line = sent.part(b, c, ROWS2 - WINDOW, ROWS2)
            moved = jnp.take_along_axis(line, own_lane[:WINDOW], axis=1)
            own_flux[c] = jnp.where(here[:WINDOW], moved, own_flux[c])
            moved = jnp.take_along_axis(line, end_lane, axis=1)
            end_flux[c] = jnp.where(there, moved, end_flux[c])
    skip = FLUX2 - (ROWS2 - WINDOW)
    later, share = count // 2, count - count // 2
    for i, parts in enumerate((own_flux, end_flux)):
        for c, start in ((0, 0), (1, later)):
            tall[2, 0:WINDOW, :] = parts[c]
            tall[i, start : start + share, :] = tall[2, skip : skip + share, :]
    iterate = surface_solve(forcing, block, lane)
    solved[...] = iterate
    rowbuf[...] = fold_take(iterate[:, 2 * rows - 1, :], block, lane)
    across_solved = rowbuf[pl.ds(me, 1), :]
    level = iota((TALL, cols), 0).astype(F32)
    fold_last = jnp.where(
        kept[TALL : TALL + 1, :] > level,
        0.25
        * v_across
        * (temp_across - kept[0:TALL, :] + th[...] * across_solved),
        0.0,
    )
    tall[2] = fold_last

    depth = depth_in[...]
    edge1_left = sent1.beside(west, EDGE1, EDGE1 + rows)
    edge1_right = sent1.beside(east, EDGE1, EDGE1 + rows)
    half = rows // 2

    def both_rows(line):
        return jnp.concatenate([line, pltpu.roll(line, cols // 2, 1)], axis=0)

    edge_left = both_rows(sent.beside(west, EDGE2, EDGE2 + half))
    edge_right = both_rows(sent.beside(east, EDGE2, EDGE2 + half))
    beside_depth = beyond1[4 * count : 4 * count + 1, :]
    masks = face_depths(depth, edge1_left, edge1_right, beside_depth, count, top)
    own, left, right, beside = load_pieces(solved, me, west, east, rows, top)
    s_out[...] = own
    pieces = (
        own,
        left,
        right,
        beside,
        lambda k: beyond[k : k + 1, :],
        lambda k: beyond1[2 * count + k : 2 * count + k + 1, :],
    )
    row = iota((rows, cols), 0)
    on_fold = (row == rows - 1) & (jnp.full((rows, cols), top.astype(jnp.int32)) == 1)

    def less(value, index, k):
        return value - jnp.where(on_fold, tall[index, k : k + 1, :], 0.0)

    def emit(k, value):
        t_out[k * rows : (k + 1) * rows, :] = less(value, 2, k)

    def spread(column):
        return jnp.broadcast_to(column, (rows, cols))

    sweep_levels(
        count,
        rows,
        th,
        lambda k: less(temp[k * rows : (k + 1) * rows, :], 0, k),
        lambda k: (
            edge1_left[:, 2 * count + k : 2 * count + k + 1],
            less(spread(edge_left[:, k : k + 1]), 1, k),
        ),
        lambda k: less(spread(edge_right[:, count + k : count + k + 1]), 1, k),
        u,
        v,
        pieces,
        top,
        depth,
        masks,
        emit,
    )


def exchange(block, peer):
    n = lax.axis_size("ia")
    rows, cols = block.shape
    kinds = [exchange_steps(n, kind) for kind in range(2)]
    y = block
    for near, far in zip(*kinds):
        pairs = []
        for i in range(n):
            for c in range(2):
                step = far if parity(i) ^ c else near
                pairs.append((2 * i + c, 2 * (i ^ step) + 1 - c))
        y = jnp.concatenate([y, lax.ppermute(y, ("ia", "ja"), pairs)])
    z = lax.ppermute(jnp.concatenate([y, peer]), "ja", [(0, 1), (1, 0)])
    both = jnp.concatenate([y, z[: n * rows]]).reshape(2, n, rows, cols)
    return both, z[n * rows :]


def on_device(
    adjoint_temp, adjoint_surface, trajectory_u, trajectory_v, levels, partner, thickness, coupling
):
    steps, count, rows, cols = trajectory_u.shape
    n = lax.axis_size("ia")
    flat = count * rows
    adj = adjoint_temp.reshape(flat, cols)
    u = trajectory_u.reshape(steps, flat, cols)
    v = trajectory_v.reshape(steps, flat, cols)
    par = partner.reshape(1, cols)

    def stay(x):
        return pltpu.with_memory_space_constraint(x, pltpu.HBM)

    vmem = pl.BlockSpec(memory_space=pltpu.VMEM)
    hbm = pl.BlockSpec(memory_space=pltpu.HBM)

    def shape(*dims):
        return jax.ShapeDtypeStruct(dims, F32)

    small = pltpu.CompilerParams(vmem_limit_bytes=(8 + n // 2) * 2**20)
    out, peer, depth, cp, th = pl.pallas_call(
        pack_kernel,
        out_shape=(
            shape(ROWS1, cols),
            shape(PEER1, cols),
            shape(rows, cols),
            shape(TALL, cols),
            shape(TALL, cols),
        ),
        in_specs=[hbm] * 8,
        out_specs=(vmem,) * 5,
        scratch_shapes=[
            pltpu.SMEM((count,), F32),
            pltpu.SMEM((count,), F32),
            pltpu.VMEM((flat, cols), F32),
            pltpu.VMEM((rows, cols), F32),
            pltpu.VMEM((steps, flat, cols), F32),
            pltpu.VMEM((steps, flat, cols), F32),
            pltpu.VMEM((rows, cols), jnp.int32),
            pltpu.VMEM((1, cols), jnp.int32),
            pltpu.SemaphoreType.DMA((8,)),
        ],
        compiler_params=small,
    )(*(stay(x) for x in (coupling, thickness, adj, adjoint_surface, u, v, levels, par)))
    both1, beyond1 = exchange(out, peer)
    temp, out, peer, kept, table = pl.pallas_call(
        first_kernel,
        out_shape=(
            shape(flat, cols),
            shape(ROWS2, cols),
            shape(PEER2, cols),
            shape(TALL + 8, cols),
            jax.ShapeDtypeStruct((n, cols), jnp.int32),
        ),
        in_specs=[vmem] * 8,
        out_specs=(vmem,) * 5,
        scratch_shapes=[
            pltpu.VMEM((n, 2 * rows, cols), F32),
            pltpu.VMEM((n, cols), F32),
            pltpu.VMEM((2, TALL, cols), F32),
        ],
        compiler_params=small,
    )(cp, th, both1, beyond1, adj, u, v, depth)
    both, beyond = exchange(out, peer)
    temp_gradient, surface_gradient = pl.pallas_call(
        second_kernel,
        out_shape=(shape(flat, cols), shape(rows, cols)),
        in_specs=[vmem] * 11,
        out_specs=(vmem, vmem),
        scratch_shapes=[
            pltpu.VMEM((n, 2 * rows, cols), F32),
            pltpu.VMEM((n, cols), F32),
            pltpu.VMEM((3, TALL, cols), F32),
        ],
        compiler_params=small,
    )(th, both, beyond, both1, beyond1, kept, table, temp, u, v, depth)
    return temp_gradient.reshape(count, rows, cols), surface_gradient


def solution(mesh):
    return jax.shard_map(
        on_device,
        mesh=mesh,
        in_specs=(
            P("grp", "ja", "ia"),
            P(("grp", "ja"), "ia"),
            P(None, None, "ja", "ia"),
            P(None, None, "ja", "ia"),
            P("ja", "ia"),
            P("ia"),
            P(),
            P(),
        ),
        out_specs=(P("grp", "ja", "ia"), P(("grp", "ja"), "ia")),
        check_vma=False,
    )
```

```python
import jax
import jax.numpy as jnp
from jax import lax
from jax.experimental import pallas as pl
from jax.experimental.pallas import tpu as pltpu
from jax.sharding import PartitionSpec as P

SOLVER_ITERS = 2
SURFACE_COEF = 2.0
F32 = jnp.float32

EDGE1, ROWS1 = 16, 32
DEPTHS = 32
EDGE2, HROW2, LINE2, FLUX2, ROWS2 = 16, 24, 25, 50, 64
PEER1, PEER2 = 104, 32
WINDOW = 16
TALL = 32


def iota(shape, dim):
    return lax.broadcasted_iota(jnp.int32, shape, dim)


def full_sum(x):
    lines = jnp.sum(x.reshape(-1, 8, x.shape[-1]), axis=0)
    return jnp.sum(jnp.sum(lines, axis=1, keepdims=True), axis=0, keepdims=True)


def split_index(column, cols):
    return column >> (cols.bit_length() - 1), column & (cols - 1)


def fold_take(values, block, lane):
    out = jnp.zeros(block.shape, F32)
    for b in range(values.shape[0]):
        source = jnp.broadcast_to(values[b : b + 1], block.shape)
        out = jnp.where(block == b, jnp.take_along_axis(source, lane, axis=1), out)
    return out


def shift_blocks(x, step):
    return jnp.concatenate([x[step:], x[:step]], axis=0)


def surface_apply(field, block, lane):
    n, rows, cols = field.shape
    col = iota(field.shape, 2)
    row = iota(field.shape, 1)
    left = pltpu.roll(field, 1, 2)
    right = pltpu.roll(field, cols - 1, 2)
    west = jnp.where(col == 0, shift_blocks(left, n - 1), left)
    east = jnp.where(col == cols - 1, shift_blocks(right, 1), right)
    across = fold_take(field[:, rows - 1, :], block, lane)
    north = jnp.where(row == rows - 1, across[:, None, :], pltpu.roll(field, rows - 1, 1))
    south = jnp.where(row == 0, 0.0, pltpu.roll(field, 1, 1))
    return (1.0 + 4.0 * SURFACE_COEF) * field - SURFACE_COEF * (east + west + north + south)


def surface_solve(forcing, block, lane):
    applied = surface_apply(forcing, block, lane)
    again = surface_apply(applied, block, lane)
    norm = full_sum(forcing * forcing)
    step_size = norm / full_sum(forcing * applied)
    residual = forcing - step_size * applied
    ratio = full_sum(residual * residual) / norm
    direction = residual + ratio * forcing
    turned = (1.0 + ratio) * applied - step_size * again
    next_size = ratio * norm / full_sum(direction * turned)
    return step_size * forcing + next_size * direction


def level_rows(ref, base, count, rows):
    return ref[pl.ds(base, count, stride=rows), :]


def code_place(rows, cols):
    return rows - 2


def start_all(pairs, sems):
    copies = [pltpu.make_async_copy(src, dst, sems.at[i]) for i, (src, dst) in enumerate(pairs)]
    for copy in copies:
        copy.start()
    return copies


def pack_kernel(
    cp_in, th_in, adj_in, surf_in, u_in, v_in, lev_in, par_in, out, peer, depth_out, cp_out, th_out,
    cp, th, adj, surf, u, v, lev, par, sems
):
    copies = start_all(
        ((cp_in, cp), (lev_in, lev), (surf_in, surf), (par_in, par), (adj_in, adj), (u_in, u), (v_in, v), (th_in, th)),
        sems,
    )
    for copy in copies[:5]:
        copy.wait()
    rows, cols = surf.shape
    count = adj.shape[0] // rows
    top = lax.axis_index("ja") == lax.axis_size("ja") - 1
    lane = iota((rows, cols), 1)
    depth = lev[...].astype(F32)
    depth_out[...] = depth
    forcing = surf[...]
    last = cols - 1
    edge = jnp.where(lane == 4 * count, depth[:, last:], 0.0)
    edge = jnp.where(lane == 4 * count + 1, depth[:, :1], edge)
    for k in range(count):
        here = adj[k * rows : (k + 1) * rows, :]
        forcing = forcing + cp[k] * jnp.where(depth > k, here, 0.0)
        edge = jnp.where(lane == k, here[:, last:], edge)
        edge = jnp.where(lane == 3 * count + k, here[:, :1], edge)
    copies[5].wait()
    for k in range(count):
        u0 = u[0, k * rows : (k + 1) * rows, :]
        u1 = u[1, k * rows : (k + 1) * rows, :]
        edge = jnp.where(lane == count + k, u1[:, last:], edge)
        edge = jnp.where(lane == 2 * count + k, u0[:, last:], edge)
    width = cols // rows
    code = par[...].astype(F32) * DEPTHS + depth[rows - 1 :]
    taken = (iota((rows, cols), 0) * width + (lane & (width - 1))) & (cols - 1)
    spread = jnp.take_along_axis(jnp.broadcast_to(code, (rows, cols)), taken, axis=1)
    edge = jnp.where(lane // width == code_place(rows, cols), spread, edge)
    out[EDGE1 : EDGE1 + rows, :] = edge
    for copy in copies[6:]:
        copy.wait()
    cp_out[...] = level_column(cp, count, cols)
    th_out[...] = level_column(th, count, cols)
    out[0:rows, :] = forcing
    peer[...] = jnp.zeros(peer.shape, F32)
    is_top = jnp.full((count, cols), top.astype(jnp.int32)) == 1
    last_row = level_rows(adj, rows - 1, count, rows)
    peer[0:count, :] = jnp.where(is_top, level_rows(adj, 0, count, rows), last_row)
    peer[count : 2 * count, :] = v[1, pl.ds(rows - 1, count, stride=rows), :]
    peer[2 * count : 3 * count, :] = v[0, pl.ds(rows - 1, count, stride=rows), :]
    peer[3 * count : 4 * count, :] = last_row
    peer[4 * count : 4 * count + 1, :] = jnp.where(is_top[:1], depth[:1], depth[rows - 1 :])


def parity(x):
    for shift in (8, 4, 2, 1):
        x = x ^ (x >> shift)
    return x & 1


def exchange_steps(n, kind):
    steps = []
    while n > 1:
        n //= 2
        steps.append(n)
    return steps if kind == 0 else steps[:1] + steps[:0:-1]


def slot_of(distance, n, kind):
    out = 0
    for r, step in enumerate(exchange_steps(n, kind)):
        out = out | (((distance >> (step.bit_length() - 1)) & 1) << r)
    return out


class Messages:
    def __init__(self, both):
        self.both = both
        self.count = both.shape[1]
        self.me = lax.axis_index("ia")
        self.kind = parity(self.me) ^ lax.axis_index("ja")
        self.own = [slot_of(self.me, self.count, kind) for kind in range(2)]

    def part(self, block, core, start, stop):
        kind = parity(block) ^ core
        slot = self.own[kind] ^ slot_of(block, self.count, kind)
        return self.both[self.kind ^ kind, slot, start:stop, :]

    def beside(self, block, start, stop):
        kind = parity(block) ^ lax.axis_index("ja")
        away = block ^ self.me
        slot = jnp.where(
            kind == 0, slot_of(away, self.count, 0), slot_of(away, self.count, 1)
        )
        return self.both[self.kind ^ kind, slot, start:stop, :]

    def field(self, rows):
        blocks = [
            jnp.concatenate([self.part(b, 0, 0, rows), self.part(b, 1, 0, rows)], axis=0)
            for b in range(self.count)
        ]
        return jnp.stack(blocks, axis=0)

    def codes(self, rows, out):
        cols = self.both.shape[3]
        width = cols // rows
        lane = iota((rows, cols), 1)
        taken = code_place(rows, cols) * width + (lane & (width - 1))
        here = lane // width == iota((rows, cols), 0)
        for b in range(self.count):
            edge = self.part(b, 1, EDGE1, EDGE1 + rows)
            moved = jnp.where(here, jnp.take_along_axis(edge, taken, axis=1), 0.0)
            out[b : b + 1, :] = jnp.sum(moved, axis=0, keepdims=True)
        return out[...].astype(jnp.int32)

    def line(self, core, index, out):
        for b in range(self.count):
            out[b : b + 1, :] = self.part(b, core, index, index + 1)
        return out[...]


def level_column(values, count, cols):
    level = iota((TALL, cols), 0)
    out = jnp.zeros((TALL, cols), F32)
    for k in range(count):
        out = jnp.where(level == k, values[k], out)
    return out


def position(n):
    me = lax.axis_index("ia")
    return me, lax.rem(me + n - 1, n), lax.rem(me + 1, n)


def sweep_levels(count, rows, th, fetch, west_of, east_of, u, v, pieces, top, depth, masks, emit):
    own, left, right, beside, beside_temp, beside_v = pieces
    east_depth, west_depth, north_depth, south_depth = masks
    cols = own.shape[1]
    lane = iota((rows, cols), 1)
    row = iota((rows, cols), 0)
    is_top = jnp.full((1, cols), top.astype(jnp.int32)) == 1
    for k in range(count):
        here = fetch(k)
        weight = th[k : k + 1, :]
        add = weight * own
        mid = here + jnp.where(depth > k, add, 0.0)
        bare = here + add
        u_west, t_west = west_of(k)
        west_value = t_west + weight * left
        east_value = jnp.where(
            lane == cols - 1, east_of(k) + weight * right, pltpu.roll(bare, cols - 1, 1)
        )
        u_here = u[k * rows : (k + 1) * rows, :]
        v_here = v[k * rows : (k + 1) * rows, :]
        flux_east = jnp.where(east_depth > k, 0.25 * u_here * (east_value - bare), 0.0)
        flux_first = jnp.where(west_depth > k, 0.25 * u_west * (bare - west_value), 0.0)
        flux_west = jnp.where(lane == 0, flux_first, pltpu.roll(flux_east, 1, 1))
        beside_value = beside_temp(k) + weight * beside
        above = jnp.where(is_top, 0.0, beside_value)
        north_value = jnp.where(row == rows - 1, above, pltpu.roll(bare, rows - 1, 0))
        flux_north = jnp.where(north_depth > k, 0.25 * v_here * (north_value - bare), 0.0)
        flux_below = jnp.where(south_depth > k, 0.25 * beside_v(k) * (bare[:1] - beside_value), 0.0)
        flux_south = jnp.where(row == 0, flux_below, pltpu.roll(flux_north, 1, 0))
        emit(k, mid + flux_east + flux_west + flux_north + flux_south)


def face_depths(depth, edge_left, edge_right, beside_depth, count, top):
    rows, cols = depth.shape
    lane = iota(depth.shape, 1)
    row = iota(depth.shape, 0)
    is_top = jnp.full(depth.shape, top.astype(jnp.int32)) == 1
    right = edge_right[:, 4 * count + 1 : 4 * count + 2]
    east = jnp.minimum(depth, jnp.where(lane == cols - 1, right, pltpu.roll(depth, cols - 1, 1)))
    west = jnp.minimum(depth, edge_left[:, 4 * count : 4 * count + 1])
    above = jnp.where(is_top, depth, beside_depth)
    north = jnp.minimum(depth, jnp.where(row == rows - 1, above, pltpu.roll(depth, rows - 1, 0)))
    south = jnp.where(is_top[:1], jnp.minimum(depth[:1], beside_depth), 0.0)
    return east, west, north, south


def load_pieces(solved, me, west, east, rows, top):
    cols = solved.shape[-1]
    here = pl.ds(pl.multiple_of(jnp.where(top, rows, 0), 8), rows)
    own = solved[me, here, :]
    left = pltpu.roll(solved[west, here, :], 1, 1)
    right = pltpu.roll(solved[east, here, :], cols - 1, 1)
    is_top = jnp.full((1, cols), top.astype(jnp.int32)) == 1
    block = solved[me]
    beside = jnp.where(is_top, block[rows - 1 : rows], block[rows : rows + 1])
    return own, left, right, beside


def first_kernel(
    cp, th, both, beyond, adj, u_in, v_in, depth_in, t_out, out, peer, kept, table, solved, rowbuf, tall
):
    u, v = u_in.at[1], v_in.at[1]
    rows, cols = depth_in.shape
    count = adj.shape[0] // rows
    top = lax.axis_index("ja") == lax.axis_size("ja") - 1
    sent = Messages(both)
    me, west, east = position(sent.count)
    code = sent.codes(rows, rowbuf)
    partner = code >> (DEPTHS.bit_length() - 1)
    table[...] = partner
    block, lane = split_index(partner, cols)
    depths = (code & (DEPTHS - 1)).astype(F32)
    rowbuf[...] = depths
    fold_depth = rowbuf[pl.ds(me, 1), :]
    rowbuf[...] = fold_take(depths, block, lane)
    across_depth = rowbuf[pl.ds(me, 1), :]

    is_top = jnp.full((count, cols), top.astype(jnp.int32)) == 1
    level = iota((TALL, cols), 0).astype(F32)
    tall[0, 0:count, :] = jnp.where(
        is_top, level_rows(v, rows - 1, count, rows), beyond[count : 2 * count, :]
    )
    tall[1, 0:count, :] = jnp.where(
        is_top, level_rows(adj, rows - 1, count, rows), beyond[3 * count : 4 * count, :]
    )
    solved[...] = surface_solve(sent.field(rows), block, lane)
    fold_solved = solved[me, 2 * rows - 8 :, :][7:]
    flux = jnp.where(
        fold_depth > level,
        0.25 * tall[0] * (tall[1] + th[...] * fold_solved),
        0.0,
    )
    into = jnp.where(across_depth > level, cp[...] * flux, 0.0)
    kept[0:TALL, :] = flux
    kept[TALL:, :] = jnp.broadcast_to(across_depth, (8, cols))
    out[HROW2 : HROW2 + 1, :] = jnp.sum(into, axis=0, keepdims=True)

    depth = depth_in[...]
    edge_left = sent.beside(west, EDGE1, EDGE1 + rows)
    edge_right = sent.beside(east, EDGE1, EDGE1 + rows)
    beside_depth = beyond[4 * count : 4 * count + 1, :]
    masks = face_depths(depth, edge_left, edge_right, beside_depth, count, top)
    own, left, right, beside = load_pieces(solved, me, west, east, rows, top)
    pieces = (
        own,
        left,
        right,
        beside,
        lambda k: beyond[k : k + 1, :],
        lambda k: beyond[count + k : count + k + 1, :],
    )
    spot = iota((rows, cols), 1)
    carry = {"forcing": own, "edge": jnp.zeros((rows, cols), F32)}

    def emit(k, value):
        t_out[k * rows : (k + 1) * rows, :] = value
        carry["forcing"] = carry["forcing"] + cp[k : k + 1, :] * jnp.where(depth > k, value, 0.0)
        edge = jnp.where(spot == k, value[:, cols - 1 :], carry["edge"])
        carry["edge"] = jnp.where(spot == count + k, value[:, :1], edge)

    sweep_levels(
        count,
        rows,
        th,
        lambda k: adj[k * rows : (k + 1) * rows, :],
        lambda k: (edge_left[:, count + k : count + k + 1], edge_left[:, k : k + 1]),
        lambda k: edge_right[:, 3 * count + k : 3 * count + k + 1],
        u,
        v,
        pieces,
        top,
        depth,
        masks,
        emit,
    )
    out[0:rows, :] = carry["forcing"]
    half = rows // 2
    edge = carry["edge"]
    out[EDGE2 : EDGE2 + half, :] = jnp.where(
        spot[:half] < cols // 2, edge[:half], pltpu.roll(edge[half:], cols // 2, 1)
    )
    last_row = level_rows(t_out, rows - 1, count, rows)
    out[LINE2 : LINE2 + count, :] = jnp.where(is_top, last_row, beyond[2 * count : 3 * count, :])
    later, share = count // 2, count - count // 2
    out[FLUX2 : FLUX2 + share, :] = jnp.where(
        is_top[:share], kept[later:count, :], kept[0:share, :]
    )
    out[FLUX2 + share :, :] = jnp.zeros((ROWS2 - FLUX2 - share, cols), F32)
    peer[0:count, :] = jnp.where(is_top, level_rows(t_out, 0, count, rows), last_row)
    peer[count:, :] = jnp.zeros((peer.shape[0] - count, cols), F32)


def second_kernel(
    th, both, beyond, both1, beyond1, kept, table, temp, u_in, v_in, depth_in, t_out, s_out, solved, rowbuf, tall
):
    u, v = u_in.at[0], v_in.at[0]
    rows, cols = depth_in.shape
    count = temp.shape[0] // rows
    top = lax.axis_index("ja") == lax.axis_size("ja") - 1
    sent, sent1 = Messages(both), Messages(both1)
    n = sent.count
    me, west, east = position(n)
    partner = table[...]
    block, lane = split_index(partner, cols)
    forcing = sent.field(rows)
    fold = fold_take(sent.line(0, HROW2, rowbuf), block, lane)
    row3 = iota(forcing.shape, 1)
    forcing = forcing - jnp.where(row3 == 2 * rows - 1, fold[:, None, :], 0.0)
    spot = iota((1, cols), 1)
    rowbuf[...] = partner.astype(F32)
    beside_left = pltpu.roll(rowbuf[pl.ds(west, 1), :], 1, 1)
    beside_right = pltpu.roll(rowbuf[pl.ds(east, 1), :], cols - 1, 1)
    end_partner = jnp.where(spot == 0, beside_left, beside_right)
    end_partner = jnp.where((spot == 0) | (spot == cols - 1), end_partner, 0.0)
    own_partner = jnp.broadcast_to(rowbuf[pl.ds(me, 1), :], (TALL, cols)).astype(jnp.int32)
    end_partner = jnp.broadcast_to(end_partner, (WINDOW, cols)).astype(jnp.int32)
    own_block, own_lane = split_index(own_partner, cols)
    end_block, end_lane = split_index(end_partner, cols)
    zero, low = jnp.zeros((TALL, cols), F32), jnp.zeros((WINDOW, cols), F32)
    temp_across, v_across = zero, zero
    own_flux, end_flux = [low, low], [low, low]
    for b in range(n):
        here, there = own_block == b, end_block == b
        line = sent.part(b, 1, LINE2, LINE2 + TALL)
        temp_across = jnp.where(here, jnp.take_along_axis(line, own_lane, axis=1), temp_across)
        line = sent.part(b, 0, LINE2, LINE2 + TALL)
        v_across = jnp.where(here, jnp.take_along_axis(line, own_lane, axis=1), v_across)
        for c in range(2):
            line = sent.part(b, c, ROWS2 - WINDOW, ROWS2)
            moved = jnp.take_along_axis(line, own_lane[:WINDOW], axis=1)
            own_flux[c] = jnp.where(here[:WINDOW], moved, own_flux[c])
            moved = jnp.take_along_axis(line, end_lane, axis=1)
            end_flux[c] = jnp.where(there, moved, end_flux[c])
    skip = FLUX2 - (ROWS2 - WINDOW)
    later, share = count // 2, count - count // 2
    for i, parts in enumerate((own_flux, end_flux)):
        for c, start in ((0, 0), (1, later)):
            tall[2, 0:WINDOW, :] = parts[c]
            tall[i, start : start + share, :] = tall[2, skip : skip + share, :]
    depth = depth_in[...]
    edge1_left = sent1.beside(west, EDGE1, EDGE1 + rows)
    edge1_right = sent1.beside(east, EDGE1, EDGE1 + rows)
    half = rows // 2

    def both_rows(line):
        return jnp.concatenate([line, pltpu.roll(line, cols // 2, 1)], axis=0)

    edge_left = both_rows(sent.beside(west, EDGE2, EDGE2 + half))
    edge_right = both_rows(sent.beside(east, EDGE2, EDGE2 + half))
    beside_depth = beyond1[4 * count : 4 * count + 1, :]
    masks = face_depths(depth, edge1_left, edge1_right, beside_depth, count, top)
    iterate = surface_solve(forcing, block, lane)
    solved[...] = iterate
    rowbuf[...] = fold_take(iterate[:, 2 * rows - 1, :], block, lane)
    across_solved = rowbuf[pl.ds(me, 1), :]
    level = iota((TALL, cols), 0).astype(F32)
    fold_last = jnp.where(
        kept[TALL : TALL + 1, :] > level,
        0.25
        * v_across
        * (temp_across - kept[0:TALL, :] + th[...] * across_solved),
        0.0,
    )
    tall[2] = fold_last

    own, left, right, beside = load_pieces(solved, me, west, east, rows, top)
    s_out[...] = own
    pieces = (
        own,
        left,
        right,
        beside,
        lambda k: beyond[k : k + 1, :],
        lambda k: beyond1[2 * count + k : 2 * count + k + 1, :],
    )
    row = iota((rows, cols), 0)
    on_fold = (row == rows - 1) & (jnp.full((rows, cols), top.astype(jnp.int32)) == 1)

    def less(value, index, k):
        return value - jnp.where(on_fold, tall[index, k : k + 1, :], 0.0)

    def emit(k, value):
        t_out[k * rows : (k + 1) * rows, :] = less(value, 2, k)

    def spread(column):
        return jnp.broadcast_to(column, (rows, cols))

    sweep_levels(
        count,
        rows,
        th,
        lambda k: less(temp[k * rows : (k + 1) * rows, :], 0, k),
        lambda k: (
            edge1_left[:, 2 * count + k : 2 * count + k + 1],
            less(spread(edge_left[:, k : k + 1]), 1, k),
        ),
        lambda k: less(spread(edge_right[:, count + k : count + k + 1]), 1, k),
        u,
        v,
        pieces,
        top,
        depth,
        masks,
        emit,
    )


def exchange(block, peer):
    n = lax.axis_size("ia")
    rows, cols = block.shape
    kinds = [exchange_steps(n, kind) for kind in range(2)]
    y = block
    for near, far in zip(*kinds):
        pairs = []
        for i in range(n):
            for c in range(2):
                step = far if parity(i) ^ c else near
                pairs.append((2 * i + c, 2 * (i ^ step) + 1 - c))
        y = jnp.concatenate([y, lax.ppermute(y, ("ia", "ja"), pairs)])
    z = lax.ppermute(jnp.concatenate([y, peer]), "ja", [(0, 1), (1, 0)])
    both = jnp.concatenate([y, z[: n * rows]]).reshape(2, n, rows, cols)
    return both, z[n * rows :]


def on_device(
    adjoint_temp, adjoint_surface, trajectory_u, trajectory_v, levels, partner, thickness, coupling
):
    steps, count, rows, cols = trajectory_u.shape
    n = lax.axis_size("ia")
    flat = count * rows
    adj = adjoint_temp.reshape(flat, cols)
    u = trajectory_u.reshape(steps, flat, cols)
    v = trajectory_v.reshape(steps, flat, cols)
    par = partner.reshape(1, cols)

    def stay(x):
        return pltpu.with_memory_space_constraint(x, pltpu.HBM)

    vmem = pl.BlockSpec(memory_space=pltpu.VMEM)
    hbm = pl.BlockSpec(memory_space=pltpu.HBM)

    def shape(*dims):
        return jax.ShapeDtypeStruct(dims, F32)

    small = pltpu.CompilerParams(vmem_limit_bytes=(8 + n // 2) * 2**20)
    out, peer, depth, cp, th = pl.pallas_call(
        pack_kernel,
        out_shape=(
            shape(ROWS1, cols),
            shape(PEER1, cols),
            shape(rows, cols),
            shape(TALL, cols),
            shape(TALL, cols),
        ),
        in_specs=[hbm] * 8,
        out_specs=(vmem,) * 5,
        scratch_shapes=[
            pltpu.SMEM((count,), F32),
            pltpu.SMEM((count,), F32),
            pltpu.VMEM((flat, cols), F32),
            pltpu.VMEM((rows, cols), F32),
            pltpu.VMEM((steps, flat, cols), F32),
            pltpu.VMEM((steps, flat, cols), F32),
            pltpu.VMEM((rows, cols), jnp.int32),
            pltpu.VMEM((1, cols), jnp.int32),
            pltpu.SemaphoreType.DMA((8,)),
        ],
        compiler_params=small,
    )(*(stay(x) for x in (coupling, thickness, adj, adjoint_surface, u, v, levels, par)))
    both1, beyond1 = exchange(out, peer)
    temp, out, peer, kept, table = pl.pallas_call(
        first_kernel,
        out_shape=(
            shape(flat, cols),
            shape(ROWS2, cols),
            shape(PEER2, cols),
            shape(TALL + 8, cols),
            jax.ShapeDtypeStruct((n, cols), jnp.int32),
        ),
        in_specs=[vmem] * 8,
        out_specs=(vmem,) * 5,
        scratch_shapes=[
            pltpu.VMEM((n, 2 * rows, cols), F32),
            pltpu.VMEM((n, cols), F32),
            pltpu.VMEM((2, TALL, cols), F32),
        ],
        compiler_params=small,
    )(cp, th, both1, beyond1, adj, u, v, depth)
    both, beyond = exchange(out, peer)
    temp_gradient, surface_gradient = pl.pallas_call(
        second_kernel,
        out_shape=(shape(flat, cols), shape(rows, cols)),
        in_specs=[vmem] * 11,
        out_specs=(vmem, vmem),
        scratch_shapes=[
            pltpu.VMEM((n, 2 * rows, cols), F32),
            pltpu.VMEM((n, cols), F32),
            pltpu.VMEM((3, TALL, cols), F32),
        ],
        compiler_params=small,
    )(th, both, beyond, both1, beyond1, kept, table, temp, u, v, depth)
    return temp_gradient.reshape(count, rows, cols), surface_gradient


def solution(mesh):
    return jax.shard_map(
        on_device,
        mesh=mesh,
        in_specs=(
            P("grp", "ja", "ia"),
            P(("grp", "ja"), "ia"),
            P(None, None, "ja", "ia"),
            P(None, None, "ja", "ia"),
            P("ja", "ia"),
            P("ia"),
            P(),
            P(),
        ),
        out_specs=(P("grp", "ja", "ia"), P(("grp", "ja"), "ia")),
        check_vma=False,
    )
```
